128 devices in a mesh: row: 8 (over z, core), col: 16 (over y, x).
Axes of the slice: x: 4, y: 4, z: 4, core: 2. Of those that a mesh axis runs over, the one named last changes fastest.
Arguments:
- object_slices: float32 [2, 2, 4096, 8192], P(None, None, 'row', 'col'), may hold values from -4.2 to 4.2
- probe: float32 [12, 2, 128, 128], replicated
- measured: float32 [8, 64, 128, 128], P('row', 'col'), may hold values from 0 to 2.2
- positions: int32 [2, 8, 64], P(None, 'row', 'col'), may hold values from 0 to 512, as said below
- counts: int32 [8, 16], P('row', 'col'), may hold values from 1 to 4, as said below
Outputs:
- object_next: float32 [2, 2, 4096, 8192], P(None, None, 'row', 'col')
- probe_next: float32 [12, 2, 128, 128], replicated
The draws below stay inside these ranges and needn't reach their ends.
Inputs may be any that keep to these rules, and one draw needn't show every extreme that they name: `positions`: row offsets are at most 512 and column offsets at most 512; in the last tile row row offsets are at most 384, in the last tile column column offsets at most 384, so each window lies within its tile and the first 128 rows and columns of the tiles below and to the right. Only the first counts[r, c] slots of a tile are live.
All inputs are finite; a program needn't handle non-finite values.
Results may differ from the reference program's by a relative error of at most 0.0003.
Values sent between devices are 32-bit elements; how exact they have to be, the bound alone decides.
No kernel may reach another device: no remote copies, remote signals or barrier semaphores. Data moves between devices by JAX's collectives and lax.ppermute only.
A program may use at most 320 MiB of HBM per device.

```python
import math
import jax
import jax.numpy as jnp
from jax import lax

PW = 128
MODES = 12
SLICES = 2
TH = 512
TW = 512
CAP = 4
OH = 4096
OW = 8192
N_ROW = 8
N_COL = 16


def draw_probe(key, part):
    key = jax.random.fold_in(key, 41)
    common_key, own_key, scale_key = jax.random.split(key, 3)
    common = jax.random.normal(common_key, (1, 2, PW, PW), jnp.float32)
    own_part = jax.random.normal(own_key, (MODES, 2, PW, PW), jnp.float32)
    low_scale, high_scale = (0.12, 0.4)
    scales = jnp.exp(jax.random.uniform(scale_key, (MODES, 1, 1, 1), jnp.float32, math.log(low_scale), math.log(high_scale)))
    return (scales * (0.6 * common + own_part)).astype(jnp.float32)


def draw_counts(key, part):
    key = jax.random.fold_in(key, 17)
    base_key, extra_key, pick_key, low_key = jax.random.split(key, 4)
    devices = N_ROW * N_COL
    base_counts = jax.random.randint(base_key, (N_ROW, N_COL), 1, CAP // 2 + 1)
    extra_full = jax.random.randint(extra_key, (N_ROW, N_COL), 0, 8) == 0
    chosen = jax.random.randint(pick_key, (), 0, devices)
    lowest = (chosen + 1 + jax.random.randint(low_key, (), 0, devices - 1)) % devices
    grid_index = jnp.arange(devices, dtype=jnp.int32).reshape(N_ROW, N_COL)
    filled = jnp.where(extra_full | (grid_index == chosen), CAP, base_counts)
    return jnp.where(grid_index == lowest, 1, filled).astype(jnp.int32)


def draw_positions(key, part):
    key = jax.random.fold_in(key, 29)
    top_key, left_key, row_key, col_key = jax.random.split(key, 4)
    grid_shape = (N_ROW, N_COL * CAP)
    row_dev = jnp.broadcast_to(jnp.arange(N_ROW, dtype=jnp.int32)[:, None], grid_shape)
    column_ids = jnp.arange(N_COL * CAP, dtype=jnp.int32)
    col_dev = jnp.broadcast_to((column_ids // CAP)[None, :], grid_shape)
    slot_no = jnp.broadcast_to((column_ids % CAP)[None, :], grid_shape)
    top_high = jnp.where(row_dev == N_ROW - 1, TH - PW + 1, TH + 1)
    left_high = jnp.where(col_dev == N_COL - 1, TW - PW + 1, TW + 1)
    top_rows = jax.random.randint(top_key, grid_shape, 0, top_high)
    left_cols = jax.random.randint(left_key, grid_shape, 0, left_high)
    pick_row = jax.random.randint(row_key, (), 0, N_ROW - 1)
    pick_col = jax.random.randint(col_key, (), 0, N_COL - 1)
    picked = (row_dev == pick_row) & (col_dev == pick_col)
    top_rows = jnp.where(picked & (slot_no == 0), TH, jnp.where(picked & (slot_no == 1), 0, top_rows))
    left_cols = jnp.where(picked & (slot_no == 0), TW, jnp.where(picked & (slot_no == 1), 0, left_cols))
    return jnp.stack([top_rows, left_cols]).astype(jnp.int32)


def block_levels(key, extent, cuts, smallest, largest):
    def one(dim, parts):
        heights = jax.random.uniform(jax.random.fold_in(jax.random.fold_in(key, 6), dim), (parts,), jnp.float32, smallest / len(cuts), largest / len(cuts))
        return jnp.repeat(jnp.exp(heights), extent[dim] // parts).reshape((-1,) + (1,) * (len(extent) - dim - 1))

    loudness = one(*cuts[0])
    for cut in cuts[1:]:
        loudness = loudness * one(*cut)
    return loudness


def centred(rng, shape, spread, limit, pieces=(), held_as=jnp.bfloat16):
    result = spread * jax.random.normal(rng, shape, jnp.float32)
    if pieces:
        result = result * block_levels(rng, shape, pieces, -0.22, 0.18)
    return jnp.clip(result, -limit, limit).astype(held_as)


def setup_inputs(seed: int = 0) -> dict:
    keys = jax.random.split(jax.random.key(seed), 6)
    return {
        "object_slices": centred(keys[0], (SLICES, 2, OH, OW), 0.7, 4.2, ((2, 8), (3, 16)), jnp.float32),
        "probe": draw_probe(jax.random.fold_in(keys[5], 71), 0),
        "measured": jnp.clip(2.2 * jax.random.uniform(keys[2], (N_ROW, N_COL * CAP, PW, PW), jnp.float32) ** block_levels(keys[2], (N_ROW, N_COL * CAP, PW, PW), ((0, 8), (1, 16)), -0.2, 0.2), 0.0, 2.2),
        "positions": draw_positions(jax.random.fold_in(keys[5], 71), 0),
        "counts": draw_counts(jax.random.fold_in(keys[5], 71), 0),
    }


FRESNEL = 40.0
highest = lax.Precision.HIGHEST

def make_tables(width):
    grid_index = jnp.arange(width, dtype=jnp.int32)
    product = grid_index[:, None] * grid_index[None, :] % width
    angles = -2.0 * math.pi / width * product.astype(jnp.float32)
    scaling = 1.0 / math.sqrt(width)
    four_re = jnp.cos(angles) * scaling
    four_im = jnp.sin(angles) * scaling
    frequency = jnp.where(grid_index < width // 2, grid_index, grid_index - width).astype(jnp.float32) / width
    phases = -FRESNEL * (frequency[:, None] ** 2 + frequency[None, :] ** 2)
    return (four_re, four_im, jnp.cos(phases), jnp.sin(phases))

def along_last(values, matrix):
    return jnp.einsum('...yk,kx->...yx', values, matrix, precision=highest)

def along_rows(values, matrix):
    return jnp.einsum('yk,...kx->...yx', matrix, values, precision=highest)

def transform(real_part, imag_part, four_re, four_im):
    rows_re = along_last(real_part, four_re) - along_last(imag_part, four_im)
    rows_im = along_last(real_part, four_im) + along_last(imag_part, four_re)
    cols_re = along_rows(rows_re, four_re) - along_rows(rows_im, four_im)
    cols_im = along_rows(rows_re, four_im) + along_rows(rows_im, four_re)
    return (cols_re, cols_im)

def complex_mul(left_re, left_im, right_re, right_im):
    return (left_re * right_re - left_im * right_im, left_re * right_im + left_im * right_re)

def propagate(real_part, imag_part, tables, direction):
    four_re, four_im, prop_re, prop_im = tables
    spec_re, spec_im = transform(real_part, imag_part, four_re, four_im)
    spec_re, spec_im = complex_mul(spec_re, spec_im, prop_re, direction * prop_im)
    return transform(spec_re, spec_im, four_re, -four_im)

def slot_terms(window, pattern, probe, tables):
    four_re, four_im = (tables[0], tables[1])
    slices = window.shape[0]
    wave_re, wave_im = (probe[:, 0], probe[:, 1])
    incoming = []
    for layer_no in range(slices):
        incoming.append((wave_re, wave_im))
        exit_re, exit_im = complex_mul(wave_re, wave_im, window[layer_no, 0], window[layer_no, 1])
        if layer_no + 1 < slices:
            wave_re, wave_im = propagate(exit_re, exit_im, tables, 1.0)
    far_re, far_im = transform(exit_re, exit_im, four_re, four_im)
    residual = lax.optimization_barrier(jnp.sum(far_re * far_re + far_im * far_im, axis=0)) - pattern
    back_re, back_im = transform(residual * far_re, residual * far_im, four_re, -four_im)
    slice_terms = [None] * slices
    for layer_no in reversed(range(slices)):
        input_re, input_im = incoming[layer_no]
        slice_terms[layer_no] = jnp.stack([lax.optimization_barrier(jnp.sum(input_re * back_re + input_im * back_im, axis=0)), lax.optimization_barrier(jnp.sum(input_re * back_im - input_im * back_re, axis=0))])
        back_re, back_im = complex_mul(back_re, back_im, window[layer_no, 0], -window[layer_no, 1])
        if layer_no > 0:
            back_re, back_im = propagate(back_re, back_im, tables, -1.0)
    return (jnp.stack(slice_terms), jnp.stack([back_re, back_im], axis=1))

def inner_sum(left_part, right_part):
    return jnp.einsum('jp,kp->jk', left_part, right_part, precision=highest)

def gram_parts(flattened):
    real_part, imag_part = (flattened[:, 0], flattened[:, 1])
    gram_re = inner_sum(real_part, real_part) + inner_sum(imag_part, imag_part)
    gram_im = inner_sum(real_part, imag_part) - inner_sum(imag_part, real_part)
    return (gram_re, gram_im)

def mode_coefficients(gram_re, gram_im):
    modes = gram_re.shape[0]
    zero_val = jnp.zeros_like(gram_re[0, 0])
    one_val = jnp.ones_like(gram_re[0, 0])
    lower = [[(zero_val, zero_val) for col_no in range(modes)] for row_no in range(modes)]
    for col_no in range(modes):
        pivot_sq = gram_re[col_no, col_no]
        for inner in range(col_no):
            entry_re, entry_im = lower[col_no][inner]
            pivot_sq = pivot_sq - (entry_re * entry_re + entry_im * entry_im)
        pivot = jnp.sqrt(pivot_sq)
        lower[col_no][col_no] = (pivot, zero_val)
        for row_no in range(col_no + 1, modes):
            value_re = gram_re[row_no, col_no]
            value_im = gram_im[row_no, col_no]
            for inner in range(col_no):
                left_re, left_im = lower[row_no][inner]
                right_re, right_im = lower[col_no][inner]
                value_re = value_re - (left_re * right_re + left_im * right_im)
                value_im = value_im - (left_im * right_re - left_re * right_im)
            lower[row_no][col_no] = (value_re / pivot, value_im / pivot)
    coef = [[(zero_val, zero_val) for col_no in range(modes)] for row_no in range(modes)]
    for col_no in range(modes):
        coef[col_no][col_no] = (one_val, zero_val)
        for row_no in reversed(range(col_no)):
            acc_re, acc_im = (zero_val, zero_val)
            for inner in range(row_no + 1, col_no + 1):
                upper_re, upper_im = (lower[inner][row_no][0], -lower[inner][row_no][1])
                coef_re_val, coef_im_val = coef[inner][col_no]
                acc_re = acc_re + upper_re * coef_re_val - upper_im * coef_im_val
                acc_im = acc_im + upper_re * coef_im_val + upper_im * coef_re_val
            pivot_val = lower[row_no][row_no][0]
            coef[row_no][col_no] = (-acc_re / pivot_val, -acc_im / pivot_val)
    coef_re = jnp.stack([jnp.stack([coef[row_no][col_no][0] for col_no in range(modes)]) for row_no in range(modes)])
    coef_im = jnp.stack([jnp.stack([coef[row_no][col_no][1] for col_no in range(modes)]) for row_no in range(modes)])
    return (coef_re, coef_im)

def combine_modes(coefs, values):
    return jnp.einsum('jk,jp->kp', coefs, values, precision=highest)

def orthogonal_modes(flattened, coef_re, coef_im):
    real_part, imag_part = (flattened[:, 0], flattened[:, 1])
    out_re = combine_modes(coef_re, real_part) - combine_modes(coef_im, imag_part)
    out_im = combine_modes(coef_re, imag_part) + combine_modes(coef_im, real_part)
    return jnp.stack([out_re, out_im], axis=1)

def reference(object_slices, probe, measured, positions, counts):
    slices = object_slices.shape[0]
    modes = probe.shape[0]
    width = probe.shape[-1]
    tables = make_tables(width)
    per_row = N_COL * CAP

    def visit(carried, slot_id):
        grad_obj, grad_probe = carried
        row_dev = slot_id // per_row
        within = slot_id % per_row
        col_dev = within // CAP
        slot_no = within % CAP
        is_live = slot_no < counts[row_dev, col_dev]
        top_row = (row_dev * TH + positions[0, row_dev, within]).astype(jnp.int32)
        left_col = (col_dev * TW + positions[1, row_dev, within]).astype(jnp.int32)
        anchor = jnp.int32(0)
        window = lax.dynamic_slice(object_slices, (anchor, anchor, top_row, left_col), (slices, 2, width, width))
        pattern = lax.dynamic_slice(measured, (row_dev.astype(jnp.int32), within.astype(jnp.int32), anchor, anchor), (1, 1, width, width))[0, 0]

        def compute():
            return slot_terms(window, pattern, probe, tables)

        def skipped():
            return (jnp.zeros((slices, 2, width, width), jnp.float32), jnp.zeros_like(probe))
        obj_term, probe_term = lax.cond(is_live, compute, skipped)
        current = lax.dynamic_slice(grad_obj, (anchor, anchor, top_row, left_col), (slices, 2, width, width))
        grad_obj = lax.dynamic_update_slice(grad_obj, current + obj_term, (anchor, anchor, top_row, left_col))
        return ((grad_obj, grad_probe + probe_term), None)
    initial = (jnp.zeros_like(object_slices), jnp.zeros_like(probe))
    (grad_obj, grad_probe), unused = lax.scan(visit, initial, jnp.arange(N_ROW * N_COL * CAP, dtype=jnp.int32))
    object_next = object_slices - grad_obj
    stepped = probe - grad_probe / math.sqrt(N_ROW * N_COL * CAP)
    flattened = stepped.reshape(modes, 2, width * width)
    gram_re, gram_im = gram_parts(flattened)
    coef_re, coef_im = mode_coefficients(gram_re, gram_im)
    probe_next = orthogonal_modes(flattened, coef_re, coef_im).reshape(modes, 2, width, width)
    return (object_next, probe_next)
```

```python
import functools
import math

import jax
import jax.numpy as jnp
import numpy as np
from jax import lax
from jax.experimental import pallas as pl
from jax.experimental.pallas import tpu as pltpu
from jax.sharding import PartitionSpec as P

FRESNEL = 40.0
f32 = jnp.float32
bf16 = jnp.bfloat16


def complex_block(matrix):
    return np.block([[matrix.real, matrix.imag], [-matrix.imag, matrix.real]])


def split_table(block):
    block = block.astype(np.float32)
    high = block.astype(jnp.bfloat16)
    low = (block - high.astype(np.float32)).astype(jnp.bfloat16)
    return np.stack([high, low])


def make_tables(width):
    index = np.arange(width)
    fourier = np.exp(-2j * np.pi / width * (index[:, None] * index[None, :] % width)) / np.sqrt(width)
    frequency = np.where(index < width // 2, index, index - width) / width
    chirp = np.exp(-1j * FRESNEL * frequency**2)
    spread = fourier.conj() @ (chirp[:, None] * fourier)
    forward = complex_block(fourier)
    step = complex_block(spread)
    return np.stack(
        [split_table(forward), split_table(forward.T), split_table(step), split_table(step.T)]
    )


def split(values):
    high = values.astype(bf16)
    low = (values - high.astype(f32)).astype(bf16)
    return high, low


def mm(left, right):
    return jnp.dot(left, right, preferred_element_type=f32)


def times_right(planes, table):
    a_re, a_im, b_re, b_im = planes
    stacked = jnp.concatenate(
        [jnp.concatenate([a_re, a_im], axis=1), jnp.concatenate([b_re, b_im], axis=1)], axis=0
    )
    high, low = split(stacked)
    out = mm(high, table[0]) + mm(low, table[0]) + mm(high, table[1])
    w = a_re.shape[0]
    return out[:w, :w], out[:w, w:], out[w:, :w], out[w:, w:]


def times_left(planes, table):
    a_re, a_im, b_re, b_im = planes
    stacked = jnp.concatenate(
        [jnp.concatenate([a_re, b_re], axis=1), jnp.concatenate([a_im, b_im], axis=1)], axis=0
    )
    high, low = split(stacked)
    out = mm(table[0], high) + mm(table[0], low) + mm(table[1], high)
    w = a_re.shape[0]
    return out[:w, :w], out[w:, :w], out[:w, w:], out[w:, w:]


def cmul(planes, re, im):
    a_re, a_im, b_re, b_im = planes
    return (
        a_re * re - a_im * im,
        a_re * im + a_im * re,
        b_re * re - b_im * im,
        b_re * im + b_im * re,
    )


def cmul_conj(planes, re, im):
    a_re, a_im, b_re, b_im = planes
    return (
        a_re * re + a_im * im,
        a_im * re - a_re * im,
        b_re * re + b_im * im,
        b_im * re - b_re * im,
    )


def overlap(wave, grad):
    re = wave[0] * grad[0] + wave[1] * grad[1] + wave[2] * grad[2] + wave[3] * grad[3]
    im = wave[0] * grad[1] - wave[1] * grad[0] + wave[2] * grad[3] - wave[3] * grad[2]
    return re, im


D_RIGHT, D_LEFT, P_RIGHT, P_LEFT = 0, 1, 2, 3


def slots_kernel(
    group,
    count_ref, pos_ref, tile, right, below, corner, probe_ref, pattern_ref, table_ref,
    pgrad_ref, tile_out, right_out, below_out, corner_out,
    ext, nxt, win, psi, far, inten, obj, sem_in, sem_out,
):
    width = probe_ref.shape[-1]
    rows, cols = tile.shape[2:]
    pairs = probe_ref.shape[0] // 4

    def region(ref, part):
        r, c = {"tile": (0, 0), "right": (0, 1), "below": (1, 0), "corner": (1, 1)}[part]
        rs = pl.ds(rows, width) if r else pl.ds(0, rows)
        cs = pl.ds(cols, width) if c else pl.ds(0, cols)
        return ref.at[:, :, rs, cs]

    loads = [
        pltpu.make_async_copy(src, region(ext, name), sem_in.at[i])
        for i, (src, name) in enumerate(
            [(tile, "tile"), (right, "right"), (below, "below"), (corner, "corner")]
        )
    ]
    loads.append(pltpu.make_async_copy(tile, region(nxt, "tile"), sem_in.at[4]))
    for copy in loads:
        copy.start()
    nxt[:, :, 0 : rows + width, cols : cols + width] = jnp.zeros((2, 2, rows + width, width), f32)
    nxt[:, :, rows : rows + width, 0:cols] = jnp.zeros((2, 2, width, cols), f32)
    pgrad_ref[...] = jnp.zeros_like(pgrad_ref)
    for copy in loads:
        copy.wait()

    def table(which):
        return table_ref[which, 0], table_ref[which, 1]

    def load4(ref, pair):
        return tuple(ref[pair * 4 + i] for i in range(4))

    def visit(slot, carry):
        top = pos_ref[0, slot]
        left = pos_ref[1, slot]
        top8 = pl.multiple_of((top // 8) * 8, 8)
        left128 = pl.multiple_of((left // width) * width, width)
        drop_r = top - top8
        drop_c = left - left128
        for s in range(2):
            for c in range(2):
                wide = ext[s, c, pl.ds(top8, width + 8), pl.ds(left128, 2 * width)]
                wide = pltpu.roll(wide, 2 * width - drop_c, 1)[:, :width]
                win[s, c] = pltpu.roll(wide, width + 8 - drop_r, 0)[:width]
        inten[...] = jnp.zeros_like(inten)

        def forward(step, carry):
            ids = [step * group + i for i in range(group)]
            waves = [cmul(load4(probe_ref, p), win[0, 0], win[0, 1]) for p in ids]
            waves = [times_right(v, table(P_RIGHT)) for v in waves]
            waves = [times_left(v, table(P_LEFT)) for v in waves]
            for p, v in zip(ids, waves):
                for i in range(4):
                    psi[p * 4 + i] = v[i]
            waves = [cmul(v, win[1, 0], win[1, 1]) for v in waves]
            waves = [times_right(v, table(D_RIGHT)) for v in waves]
            waves = [times_left(v, table(D_LEFT)) for v in waves]
            total = inten[...]
            for p, v in zip(ids, waves):
                for i in range(4):
                    far[p * 4 + i] = v[i]
                total = total + (v[0] * v[0] + v[1] * v[1] + v[2] * v[2] + v[3] * v[3])
            inten[...] = total
            return carry

        lax.fori_loop(0, pairs // group, forward, 0)
        inten[...] = inten[...] - pattern_ref[slot]
        obj[...] = jnp.zeros_like(obj)

        def backward(step, carry):
            ids = [step * group + i for i in range(group)]
            residual = inten[...]
            grads = [tuple(residual * x for x in load4(far, p)) for p in ids]
            grads = [times_right(v, table(D_LEFT)) for v in grads]
            grads = [times_left(v, table(D_RIGHT)) for v in grads]
            for p, v in zip(ids, grads):
                re, im = overlap(load4(psi, p), v)
                obj[1, 0] += re
                obj[1, 1] += im
            grads = [cmul_conj(v, win[1, 0], win[1, 1]) for v in grads]
            grads = [times_right(v, table(P_LEFT)) for v in grads]
            grads = [times_left(v, table(P_RIGHT)) for v in grads]
            for p, v in zip(ids, grads):
                re, im = overlap(load4(probe_ref, p), v)
                obj[0, 0] += re
                obj[0, 1] += im
            grads = [cmul_conj(v, win[0, 0], win[0, 1]) for v in grads]
            for p, v in zip(ids, grads):
                for i in range(4):
                    pgrad_ref[p * 4 + i] += v[i]
            return carry

        lax.fori_loop(0, pairs // group, backward, 0)
        for s in range(2):
            for c in range(2):
                wide = jnp.concatenate([obj[s, c], jnp.zeros((8, width), f32)], axis=0)
                wide = pltpu.roll(wide, drop_r, 0)
                wide = jnp.concatenate([wide, jnp.zeros_like(wide)], axis=1)
                wide = pltpu.roll(wide, drop_c, 1)
                place = (s, c, pl.ds(top8, width + 8), pl.ds(left128, 2 * width))
                nxt[place] = nxt[place] - wide
        return carry

    lax.fori_loop(0, count_ref[0, 0], visit, 0)
    stores = [
        pltpu.make_async_copy(region(nxt, name), dst, sem_out.at[i])
        for i, (dst, name) in enumerate(
            [(tile_out, "tile"), (right_out, "right"), (below_out, "below"), (corner_out, "corner")]
        )
    ]
    for copy in stores:
        copy.start()
    for copy in stores:
        copy.wait()


def run_slots(tile, right, below, corner, probe, patterns, positions, counts, group=2):
    width = probe.shape[-1]
    rows, cols = tile.shape[2:]
    planes = 2 * probe.shape[0]
    tables = jnp.asarray(make_tables(width))
    vmem = pl.BlockSpec(memory_space=pltpu.VMEM)
    smem = pl.BlockSpec(memory_space=pltpu.SMEM)
    hbm = pl.BlockSpec(memory_space=pl.ANY)
    padded = (2, 2, rows + width + 8, cols + 2 * width)
    shapes = [
        jax.ShapeDtypeStruct((planes, width, width), f32),
        jax.ShapeDtypeStruct(tile.shape, f32),
        jax.ShapeDtypeStruct(right.shape, f32),
        jax.ShapeDtypeStruct(below.shape, f32),
        jax.ShapeDtypeStruct(corner.shape, f32),
    ]
    return pl.pallas_call(
        functools.partial(slots_kernel, group),
        out_shape=shapes,
        in_specs=[smem, smem, hbm, hbm, hbm, hbm, vmem, vmem, vmem],
        out_specs=[vmem, hbm, hbm, hbm, hbm],
        scratch_shapes=[
            pltpu.VMEM(padded, f32),
            pltpu.VMEM(padded, f32),
            pltpu.VMEM((2, 2, width, width), f32),
            pltpu.VMEM((planes, width, width), f32),
            pltpu.VMEM((planes, width, width), f32),
            pltpu.VMEM((width, width), f32),
            pltpu.VMEM((2, 2, width, width), f32),
            pltpu.SemaphoreType.DMA((5,)),
            pltpu.SemaphoreType.DMA((4,)),
        ],
        compiler_params=pltpu.CompilerParams(vmem_limit_bytes=56 * 1024 * 1024),
        name="slots",
    )(counts, positions, tile, right, below, corner, probe.reshape(planes, width, width), patterns, tables)


def core_groups(rows, cols, split):
    return [
        [r * cols + c for r in range(part, rows, split) for c in range(cols)]
        for part in range(split)
    ]


def orthogonal_kernel(scale, probe_ref, total_ref, out_ref, stepped, sums, gram, coef):
    planes, width = probe_ref.shape[0], probe_ref.shape[-1]
    modes = planes // 2
    sub = 8
    chunks = width // sub
    stepped[...] = probe_ref[...] - total_ref[...] * scale

    block = 3
    sums[...] = jnp.zeros_like(sums)
    for jb in range(0, modes, block):
        for kb in range(jb, modes, block):
            pairs = [
                (j, k) for j in range(jb, jb + block) for k in range(kb, kb + block) if j <= k
            ]

            def accumulate(chunk, carried):
                rows = pl.ds(pl.multiple_of(chunk * sub, sub), sub)
                left = {j: (stepped[2 * j, rows], stepped[2 * j + 1, rows]) for j in range(jb, jb + block)}
                right = {k: (stepped[2 * k, rows], stepped[2 * k + 1, rows]) for k in range(kb, kb + block)}
                out = []
                for (j, k), (acc_re, acc_im) in zip(pairs, carried):
                    (l_re, l_im), (r_re, r_im) = left[j], right[k]
                    out.append(
                        (
                            acc_re + l_re * r_re + l_im * r_im,
                            acc_im + l_re * r_im - l_im * r_re,
                        )
                    )
                return out

            zero = jnp.zeros((sub, width), f32)
            result = lax.fori_loop(
                0, chunks, accumulate, [(zero, zero) for _ in pairs], unroll=4
            )
            for (j, k), (acc_re, acc_im) in zip(pairs, result):
                s_re = jnp.sum(acc_re, axis=0, keepdims=True)
                s_im = jnp.sum(acc_im, axis=0, keepdims=True)
                sums[0, j, k : k + 1] = s_re
                sums[1, j, k : k + 1] = s_im
                if j != k:
                    sums[0, k, j : j + 1] = s_re
                    sums[1, k, j : j + 1] = -s_im
    side = sums.shape[1]
    ones = jnp.ones((sub, width), f32)
    for part in range(2):
        for j in range(modes):
            row = lax.dot_general(
                ones, sums[part, j], (((1,), (1,)), ((), ())),
                precision=lax.Precision.HIGHEST, preferred_element_type=f32,
            )
            gram[part, j : j + 1, 0:side] = row[0:1]

    row_id = lax.broadcasted_iota(jnp.int32, (side, width), 0)
    lane_id = lax.broadcasted_iota(jnp.int32, (side, width), 1)
    valid = (row_id < modes) & (lane_id < modes)
    eye = jnp.where((lane_id == row_id + side) & (row_id < modes), 1.0, 0.0)
    work_re = jnp.where(valid, gram[0], 0.0) + eye
    work_im = jnp.where(valid, gram[1], 0.0)
    for k in range(modes - 1):
        row_re = work_re[k : k + 1]
        row_im = work_im[k : k + 1]
        inverse = 1.0 / work_re[k : k + 1, k : k + 1]
        f_re = jnp.where(row_id[:, :1] > k, work_re[:, k : k + 1] * inverse, 0.0)
        f_im = jnp.where(row_id[:, :1] > k, work_im[:, k : k + 1] * inverse, 0.0)
        work_re, work_im = (
            work_re - (f_re * row_re - f_im * row_im),
            work_im - (f_re * row_im + f_im * row_re),
        )
    place = 0
    for k in range(modes):
        for j in range(k):
            coef[place] = jnp.broadcast_to(work_re[k : k + 1, side + j : side + j + 1], (sub, width))
            coef[place + 1] = jnp.broadcast_to(work_im[k : k + 1, side + j : side + j + 1], (sub, width))
            place += 2

    def combine(chunk, carry):
        rows = pl.ds(pl.multiple_of(chunk * sub, sub), sub)
        values = [stepped[i, rows] for i in range(planes)]
        place = 0
        for k in range(modes):
            acc_re, acc_im = values[2 * k], values[2 * k + 1]
            for j in range(k):
                c_re, c_im = coef[place], coef[place + 1]
                place += 2
                acc_re = acc_re + (c_re * values[2 * j] + c_im * values[2 * j + 1])
                acc_im = acc_im + (c_re * values[2 * j + 1] - c_im * values[2 * j])
            out_ref[2 * k, rows] = acc_re
            out_ref[2 * k + 1, rows] = acc_im
        return carry

    lax.fori_loop(0, chunks, combine, 0)


def orthogonalize(probe, total, divisor):
    planes, width = probe.shape[0], probe.shape[-1]
    modes = planes // 2
    side = 16
    vmem = pl.BlockSpec(memory_space=pltpu.VMEM)
    return pl.pallas_call(
        functools.partial(orthogonal_kernel, 1.0 / divisor),
        out_shape=jax.ShapeDtypeStruct(probe.shape, f32),
        in_specs=[vmem, vmem],
        out_specs=vmem,
        scratch_shapes=[
            pltpu.VMEM(probe.shape, f32),
            pltpu.VMEM((2, side, side, width), f32),
            pltpu.VMEM((2, side, width), f32),
            pltpu.VMEM((modes * (modes - 1), 8, width), f32),
        ],
        compiler_params=pltpu.CompilerParams(vmem_limit_bytes=32 * 1024 * 1024),
        name="orthogonalize",
    )(probe, total)


def moved(shard, axes, pairs):
    return lax.ppermute(shard, axes, pairs)


def shifted(size, by):
    return [(i, i + by) for i in range(size) if 0 <= i + by < size]


def shifted_both(rows, cols, by):
    return [
        (r * cols + c, (r + by) * cols + c + by)
        for r in range(rows)
        for c in range(cols)
        if 0 <= r + by < rows and 0 <= c + by < cols
    ]


def total_over_devices(own, rows, cols):
    planes, width = own.shape[0], own.shape[-1]
    core = lax.axis_index("row") % 2
    swap = [(r, r ^ 1) for r in range(rows)]
    halves = own.reshape(2, planes // 2 * width, width)
    keep = lax.dynamic_index_in_dim(halves, core, 0, keepdims=False)
    give = lax.dynamic_index_in_dim(halves, 1 - core, 0, keepdims=False)
    keep = keep + moved(give, "row", swap)
    members = rows * cols // 2
    groups = core_groups(rows, cols, 2)
    parts = keep.reshape(members, -1, width)
    parts = lax.all_to_all(parts, ("row", "col"), 0, 0, axis_index_groups=groups)
    share = jnp.sum(parts, axis=0, keepdims=True)
    share = jnp.broadcast_to(share, parts.shape)
    mine = lax.all_to_all(share, ("row", "col"), 0, 0, axis_index_groups=groups)
    mine = mine.reshape(keep.shape)
    other = moved(mine, "row", swap)
    first = jnp.where(core == 0, mine, other)
    second = jnp.where(core == 0, other, mine)
    return jnp.concatenate([first, second]).reshape(own.shape)


def local(object_slices, probe, measured, positions, counts):
    rows, cols = lax.axis_size("row"), lax.axis_size("col")
    modes, width = probe.shape[0], probe.shape[-1]
    capacity = positions.shape[2]
    left_one, right_one = shifted(cols, -1), shifted(cols, 1)
    up_one, down_one = shifted(rows, -1), shifted(rows, 1)
    right = moved(object_slices[:, :, :, :width], "col", left_one)
    below = moved(object_slices[:, :, :width, :], "row", up_one)
    corner = moved(
        object_slices[:, :, :width, :width], ("row", "col"), shifted_both(rows, cols, -1)
    )
    probe_grad, partial, right_grad, below_grad, corner_grad = run_slots(
        object_slices, right, below, corner, probe, measured[0], positions[:, 0], counts, group=6
    )
    from_left = moved(right_grad, "col", right_one)
    from_above = moved(below_grad, "row", down_one)
    from_corner = moved(corner_grad, ("row", "col"), shifted_both(rows, cols, 1))
    total = total_over_devices(probe_grad, rows, cols)
    object_next = partial.at[:, :, :, :width].add(from_left)
    object_next = object_next.at[:, :, :width, :].add(from_above)
    object_next = object_next.at[:, :, :width, :width].add(from_corner)
    divisor = math.sqrt(rows * cols * capacity)
    planes = probe.reshape(2 * modes, width, width)
    probe_next = orthogonalize(planes, total, divisor).reshape(probe.shape)
    return (object_next, probe_next)


def solution(mesh):
    return jax.shard_map(
        local,
        mesh=mesh,
        in_specs=(
            P(None, None, "row", "col"),
            P(),
            P("row", "col", None, None),
            P(None, "row", "col"),
            P("row", "col"),
        ),
        out_specs=(P(None, None, "row", "col"), P()),
        check_vma=False,
    )
```

```python
import functools
import math

import jax
import jax.numpy as jnp
import numpy as np
from jax import lax
from jax.experimental import pallas as pl
from jax.experimental.pallas import tpu as pltpu
from jax.sharding import PartitionSpec as P

FRESNEL = 40.0
f32 = jnp.float32
bf16 = jnp.bfloat16


def complex_block(matrix):
    return np.block([[matrix.real, matrix.imag], [-matrix.imag, matrix.real]])


def split_table(block):
    block = block.astype(np.float32)
    high = block.astype(jnp.bfloat16)
    low = (block - high.astype(np.float32)).astype(jnp.bfloat16)
    return np.stack([high, low])


def make_tables(width):
    index = np.arange(width)
    fourier = np.exp(-2j * np.pi / width * (index[:, None] * index[None, :] % width)) / np.sqrt(width)
    frequency = np.where(index < width // 2, index, index - width) / width
    chirp = np.exp(-1j * FRESNEL * frequency**2)
    spread = fourier.conj() @ (chirp[:, None] * fourier)
    forward = complex_block(fourier)
    step = complex_block(spread)
    steps = np.stack([split_table(step), split_table(step.T)])
    transforms = np.stack([split_table(forward), split_table(forward.T)])
    return steps, transforms


def split(values):
    high = values.astype(bf16)
    low = (values - high.astype(f32)).astype(bf16)
    return high, low


def mm(left, right):
    return jnp.dot(left, right, preferred_element_type=f32)


def times_right(planes, table):
    a_re, a_im, b_re, b_im = planes
    stacked = jnp.concatenate(
        [jnp.concatenate([a_re, a_im], axis=1), jnp.concatenate([b_re, b_im], axis=1)], axis=0
    )
    high, low = split(stacked)
    out = mm(high, table[0]) + mm(low, table[0]) + mm(high, table[1])
    w = a_re.shape[0]
    return out[:w, :w], out[:w, w:], out[w:, :w], out[w:, w:]


def times_left(planes, table):
    a_re, a_im, b_re, b_im = planes
    stacked = jnp.concatenate(
        [jnp.concatenate([a_re, b_re], axis=1), jnp.concatenate([a_im, b_im], axis=1)], axis=0
    )
    high, low = split(stacked)
    out = mm(table[0], high) + mm(table[0], low) + mm(table[1], high)
    w = a_re.shape[0]
    return out[:w, :w], out[w:, :w], out[:w, w:], out[w:, w:]


def cmul(planes, re, im):
    a_re, a_im, b_re, b_im = planes
    return (
        a_re * re - a_im * im,
        a_re * im + a_im * re,
        b_re * re - b_im * im,
        b_re * im + b_im * re,
    )


def cmul_conj(planes, re, im):
    a_re, a_im, b_re, b_im = planes
    return (
        a_re * re + a_im * im,
        a_im * re - a_re * im,
        b_re * re + b_im * im,
        b_im * re - b_re * im,
    )


def overlap(wave, grad):
    re = wave[0] * grad[0] + wave[1] * grad[1] + wave[2] * grad[2] + wave[3] * grad[3]
    im = wave[0] * grad[1] - wave[1] * grad[0] + wave[2] * grad[3] - wave[3] * grad[2]
    return re, im


RIGHT, LEFT = 0, 1


def load_sheet(tile, halo, sheet, sems, width):
    rows, cols = tile.shape[2:]
    top, rest, below_first, below_second, corner = halo
    half = rows // 2
    spots = [
        (tile, sheet, 0, rows, 0, cols),
        (top, sheet, 0, half, cols, width),
        (rest, sheet, half, half, cols, width),
        (below_first, sheet.at[pl.ds(0, 1)], rows, width, 0, cols),
        (below_second, sheet.at[pl.ds(1, 1)], rows, width, 0, cols),
        (corner, sheet, rows, width, cols, width),
    ]
    copies = [
        pltpu.make_async_copy(src, dst.at[:, :, pl.ds(r, h), pl.ds(c, w)], sems.at[i])
        for i, (src, dst, r, h, c, w) in enumerate(spots)
    ]
    for copy in copies:
        copy.start()
    return copies


def corner_of(pos_ref, slot, width):
    top = pos_ref[0, slot]
    left = pos_ref[1, slot]
    top8 = pl.multiple_of((top // 8) * 8, 8)
    left128 = pl.multiple_of((left // width) * width, width)
    return top8, left128, top - top8, left - left128


def cut_window(sheet, layer, plane, corner, width):
    top8, left128, drop_r, drop_c = corner
    wide = sheet[layer, plane, pl.ds(top8, width + 8), pl.ds(left128, 2 * width)]
    wide = pltpu.roll(wide, 2 * width - drop_c, 1)[:, :width]
    return pltpu.roll(wide, width + 8 - drop_r, 0)[:width]


def load4(ref, pair):
    return tuple(ref[pair * 4 + i] for i in range(4))


def store4(ref, pair, values):
    for i in range(4):
        ref[pair * 4 + i] = values[i]


def subtract_terms(slot, pos_ref, terms, sheet, width):
    top8, left128, drop_r, drop_c = corner_of(pos_ref, slot, width)
    for s in range(2):
        for c in range(2):
            wide = jnp.concatenate([terms[slot, s, c], jnp.zeros((8, width), f32)], axis=0)
            wide = pltpu.roll(wide, drop_r, 0)
            wide = jnp.concatenate([wide, jnp.zeros_like(wide)], axis=1)
            wide = pltpu.roll(wide, drop_c, 1)
            where = (s, c, pl.ds(top8, width + 8), pl.ds(left128, 2 * width))
            sheet[where] = sheet[where] - wide


def slots_kernel(
    count_ref, pos_ref, core_ref, tile, top, rest, below_first, below_second, corner,
    probe_in, pattern_in, step_in, transform_in,
    keep_out, give_out, term_out, right_top_out, right_rest_out, below_first_out, below_second_out,
    corner_out,
    sheet, outer, probe, patterns, steps, transforms, window, wave, far, inten, pgrad, terms,
    sem_in, sem_load, sem_term, sem_out,
):
    rows, cols = tile.shape[2:]
    width = probe.shape[-1]
    planes = probe.shape[0]
    pairs = planes // 4
    count = count_ref[0, 0]
    copies = load_sheet(tile, (top, rest, below_first, below_second, corner), sheet, sem_in, width)
    loads = [
        pltpu.make_async_copy(src, dst, sem_load.at[i])
        for i, (src, dst) in enumerate(
            [(probe_in, probe), (step_in, steps), (transform_in, transforms), (pattern_in, patterns)]
        )
    ]
    for copy in loads:
        copy.start()

    def save(slot):
        return pltpu.make_async_copy(terms.at[slot], term_out.at[slot], sem_term.at[slot])

    pgrad[...] = jnp.zeros_like(pgrad)
    outer[:, :, 0 : rows + width, cols : cols + width] = jnp.zeros((2, 2, rows + width, width), f32)
    outer[:, :, rows : rows + width, 0:cols] = jnp.zeros((2, 2, width, cols), f32)
    for copy in copies + loads:
        copy.wait()

    def visit(slot, carry):
        place = corner_of(pos_ref, slot, width)
        for s in range(2):
            for c in range(2):
                window[s, c] = cut_window(sheet, s, c, place, width)
        waves = [cmul(load4(probe, p), window[0, 0], window[0, 1]) for p in range(pairs)]
        waves = [times_right(v, steps[RIGHT]) for v in waves]
        waves = [times_left(v, steps[LEFT]) for v in waves]
        for p, v in enumerate(waves):
            store4(wave, p, v)
        waves = [cmul(v, window[1, 0], window[1, 1]) for v in waves]
        waves = [times_right(v, transforms[RIGHT]) for v in waves]
        waves = [times_left(v, transforms[LEFT]) for v in waves]
        total = -patterns[slot]
        for p, v in enumerate(waves):
            store4(far, p, v)
            total = total + (v[0] * v[0] + v[1] * v[1] + v[2] * v[2] + v[3] * v[3])
        inten[...] = total

        residual = inten[...]
        grads = [tuple(residual * x for x in load4(far, p)) for p in range(pairs)]
        grads = [times_right(v, transforms[LEFT]) for v in grads]
        grads = [times_left(v, transforms[RIGHT]) for v in grads]
        products = [overlap(load4(wave, p), v) for p, v in enumerate(grads)]
        terms[slot, 1, 0] = sum(t[0] for t in products)
        terms[slot, 1, 1] = sum(t[1] for t in products)
        grads = [cmul_conj(v, window[1, 0], window[1, 1]) for v in grads]
        grads = [times_right(v, steps[LEFT]) for v in grads]
        grads = [times_left(v, steps[RIGHT]) for v in grads]
        products = [overlap(load4(probe, p), v) for p, v in enumerate(grads)]
        terms[slot, 0, 0] = sum(t[0] for t in products)
        terms[slot, 0, 1] = sum(t[1] for t in products)
        grads = [cmul_conj(v, window[0, 0], window[0, 1]) for v in grads]
        for p, v in enumerate(grads):
            for i in range(4):
                pgrad[p * 4 + i] += v[i]
        save(slot).start()
        leaves = (pos_ref[0, slot] > rows - width) | (pos_ref[1, slot] > cols - width)

        @pl.when(leaves)
        def _():
            subtract_terms(slot, pos_ref, terms, outer, width)

        return carry

    def finish(slot, carry):
        save(slot).wait()
        return carry

    lax.fori_loop(0, count, visit, 0)
    half = planes // 2
    core = core_ref[0, 0]
    middle = rows // 2
    down, across = pl.ds(rows, width), pl.ds(cols, width)
    results = [
        (pgrad.at[pl.ds((1 - core) * half, half)], give_out),
        (pgrad.at[pl.ds(core * half, half)], keep_out),
        (outer.at[:, :, down, across], corner_out),
        (outer.at[:, :, pl.ds(middle, middle), across], right_rest_out),
        (outer.at[:, :, pl.ds(0, middle), across], right_top_out),
        (outer.at[pl.ds(0, 1), :, down, pl.ds(0, cols)], below_first_out),
        (outer.at[pl.ds(1, 1), :, down, pl.ds(0, cols)], below_second_out),
    ]
    stores = [
        pltpu.make_async_copy(src, dst, sem_out.at[i]) for i, (src, dst) in enumerate(results)
    ]
    for copy in stores:
        copy.start()
    lax.fori_loop(0, count, finish, 0)
    for copy in stores:
        copy.wait()


def load_terms(count, term_in, terms, sems):
    def fetch(slot):
        return pltpu.make_async_copy(term_in.at[slot], terms.at[slot], sems.at[slot])

    def begin(slot, carry):
        fetch(slot).start()
        return carry

    def finish(slot, carry):
        fetch(slot).wait()
        return carry

    lax.fori_loop(0, count, begin, 0)
    return lambda: lax.fori_loop(0, count, finish, 0)


def settle_kernel(
    count_ref, pos_ref, tile, term_in, left_top_in, left_rest_in, above_first_in, above_second_in, tile_out,
    sheet, terms, left, above, sem_term, sem_in, sem_out,
):
    width = above_first_in.shape[2]
    rows, cols = tile.shape[2:]
    middle = rows // 2
    count = count_ref[0, 0]
    inner = sheet.at[:, :, pl.ds(0, rows), pl.ds(0, cols)]
    sources = [
        (tile, inner),
        (left_top_in, left.at[:, :, pl.ds(0, middle)]),
        (left_rest_in, left.at[:, :, pl.ds(middle, middle)]),
        (above_first_in, above.at[pl.ds(0, 1)]),
        (above_second_in, above.at[pl.ds(1, 1)]),
    ]
    loads = [
        pltpu.make_async_copy(src, dst, sem_in.at[i]) for i, (src, dst) in enumerate(sources)
    ]
    for copy in loads:
        copy.start()
    wait = load_terms(count, term_in, terms, sem_term)
    for copy in loads:
        copy.wait()
    wait()
    sheet[:, :, 0:rows, 0:width] += left[...]
    sheet[:, :, 0:width, 0:cols] += above[...]

    def visit(slot, carry):
        subtract_terms(slot, pos_ref, terms, sheet, width)
        return carry

    lax.fori_loop(0, count, visit, 0)
    store = pltpu.make_async_copy(inner, tile_out, sem_out.at[0])
    store.start()
    store.wait()


VMEM = pl.BlockSpec(memory_space=pltpu.VMEM)
SMEM = pl.BlockSpec(memory_space=pltpu.SMEM)
ANY = pl.BlockSpec(memory_space=pl.ANY)
DMA = pltpu.SemaphoreType.DMA


def shape(*dims):
    return jax.ShapeDtypeStruct(dims, f32)


def params(mib):
    return pltpu.CompilerParams(vmem_limit_bytes=mib * 1024 * 1024)


def work(products):
    return pl.CostEstimate(
        flops=products * 2 * 256**3, bytes_accessed=8 * 1024 * 1024, transcendentals=0
    )


def run_slots(counts, positions, core, tile, halo, probe, patterns):
    planes, width = probe.shape[0], probe.shape[-1]
    rows, cols = tile.shape[2:]
    capacity = positions.shape[1]
    half = (planes // 2, width, width)
    stack = pltpu.VMEM(probe.shape, f32)
    steps, transforms = make_tables(width)
    return pl.pallas_call(
        slots_kernel,
        out_shape=[
            shape(*half),
            shape(*half),
            shape(capacity, 2, 2, width, width),
            shape(2, 2, rows // 2, width),
            shape(2, 2, rows // 2, width),
            shape(1, 2, width, cols),
            shape(1, 2, width, cols),
            shape(2, 2, width, width),
        ],
        in_specs=[SMEM, SMEM, SMEM] + [ANY] * 10,
        out_specs=[ANY] * 8,
        scratch_shapes=[
            pltpu.VMEM((2, 2, rows + width + 8, cols + 2 * width), f32),
            pltpu.VMEM((2, 2, rows + width + 8, cols + 2 * width), f32),
            stack,
            pltpu.VMEM(patterns.shape, f32),
            pltpu.VMEM(steps.shape, bf16),
            pltpu.VMEM(transforms.shape, bf16),
            pltpu.VMEM((2, 2, width, width), f32),
            stack,
            stack,
            pltpu.VMEM((width, width), f32),
            stack,
            pltpu.VMEM((capacity, 2, 2, width, width), f32),
            DMA((6,)),
            DMA((4,)),
            DMA((capacity,)),
            DMA((7,)),
        ],
        compiler_params=params(60),
        cost_estimate=work(4 * capacity * planes),
        name="slots",
    )(counts, positions, core, tile, *halo, probe, patterns, steps, transforms)


def settle(counts, positions, tile, terms, left, above):
    capacity, width = terms.shape[0], terms.shape[-1]
    rows, cols = tile.shape[2:]
    return pl.pallas_call(
        settle_kernel,
        out_shape=shape(*tile.shape),
        in_specs=[SMEM, SMEM] + [ANY] * 6,
        out_specs=ANY,
        scratch_shapes=[
            pltpu.VMEM((2, 2, rows + width + 8, cols + 2 * width), f32),
            pltpu.VMEM(terms.shape, f32),
            pltpu.VMEM((2, 2, rows, width), f32),
            pltpu.VMEM((2, 2, width, cols), f32),
            DMA((capacity,)),
            DMA((5,)),
            DMA((1,)),
        ],
        compiler_params=params(60),
        cost_estimate=work(4096),
        name="settle",
    )(counts, positions, tile, terms, *left, *above)


def core_groups(rows, cols, split):
    return [
        [r * cols + c for r in range(part, rows, split) for c in range(cols)]
        for part in range(split)
    ]


def orthogonal_kernel(
    scale, core_ref, probe_ref, mine, other, out_ref, total, stepped, sums, gram, coef, sem
):
    planes, width = probe_ref.shape[0], probe_ref.shape[-1]
    half = planes // 2
    core = core_ref[0, 0]
    loads = [
        pltpu.make_async_copy(mine, total.at[pl.ds(core * half, half)], sem.at[0]),
        pltpu.make_async_copy(other, total.at[pl.ds((1 - core) * half, half)], sem.at[1]),
    ]
    for copy in loads:
        copy.start()
    for copy in loads:
        copy.wait()
    modes = planes // 2
    sub = 8
    chunks = width // sub
    stepped[...] = probe_ref[...] - total[...] * scale

    block = 3
    sums[...] = jnp.zeros_like(sums)
    for jb in range(0, modes, block):
        for kb in range(jb, modes, block):
            pairs = [
                (j, k) for j in range(jb, jb + block) for k in range(kb, kb + block) if j <= k
            ]

            def accumulate(chunk, carried):
                rows = pl.ds(pl.multiple_of(chunk * sub, sub), sub)
                left = {j: (stepped[2 * j, rows], stepped[2 * j + 1, rows]) for j in range(jb, jb + block)}
                right = {k: (stepped[2 * k, rows], stepped[2 * k + 1, rows]) for k in range(kb, kb + block)}
                out = []
                for (j, k), (acc_re, acc_im) in zip(pairs, carried):
                    (l_re, l_im), (r_re, r_im) = left[j], right[k]
                    out.append(
                        (
                            acc_re + l_re * r_re + l_im * r_im,
                            acc_im + l_re * r_im - l_im * r_re,
                        )
                    )
                return out

            zero = jnp.zeros((sub, width), f32)
            result = lax.fori_loop(
                0, chunks, accumulate, [(zero, zero) for _ in pairs], unroll=4
            )
            for (j, k), (acc_re, acc_im) in zip(pairs, result):
                s_re = jnp.sum(acc_re, axis=0, keepdims=True)
                s_im = jnp.sum(acc_im, axis=0, keepdims=True)
                sums[0, j, k : k + 1] = s_re
                sums[1, j, k : k + 1] = s_im
                if j != k:
                    sums[0, k, j : j + 1] = s_re
                    sums[1, k, j : j + 1] = -s_im
    side = sums.shape[1]
    ones = jnp.ones((sub, width), f32)
    for part in range(2):
        for j in range(modes):
            row = lax.dot_general(
                ones, sums[part, j], (((1,), (1,)), ((), ())),
                precision=lax.Precision.HIGHEST, preferred_element_type=f32,
            )
            gram[part, j : j + 1, 0:side] = row[0:1]

    row_id = lax.broadcasted_iota(jnp.int32, (side, width), 0)
    lane_id = lax.broadcasted_iota(jnp.int32, (side, width), 1)
    valid = (row_id < modes) & (lane_id < modes)
    eye = jnp.where((lane_id == row_id + side) & (row_id < modes), 1.0, 0.0)
    work_re = jnp.where(valid, gram[0], 0.0) + eye
    work_im = jnp.where(valid, gram[1], 0.0)
    for k in range(modes - 1):
        row_re = work_re[k : k + 1]
        row_im = work_im[k : k + 1]
        inverse = 1.0 / work_re[k : k + 1, k : k + 1]
        f_re = jnp.where(row_id[:, :1] > k, work_re[:, k : k + 1] * inverse, 0.0)
        f_im = jnp.where(row_id[:, :1] > k, work_im[:, k : k + 1] * inverse, 0.0)
        work_re, work_im = (
            work_re - (f_re * row_re - f_im * row_im),
            work_im - (f_re * row_im + f_im * row_re),
        )
    place = 0
    for k in range(modes):
        for j in range(k):
            coef[place] = jnp.broadcast_to(work_re[k : k + 1, side + j : side + j + 1], (sub, width))
            coef[place + 1] = jnp.broadcast_to(work_im[k : k + 1, side + j : side + j + 1], (sub, width))
            place += 2

    def combine(chunk, carry):
        rows = pl.ds(pl.multiple_of(chunk * sub, sub), sub)
        values = [stepped[i, rows] for i in range(planes)]
        place = 0
        for k in range(modes):
            acc_re, acc_im = values[2 * k], values[2 * k + 1]
            for j in range(k):
                c_re, c_im = coef[place], coef[place + 1]
                place += 2
                acc_re = acc_re + (c_re * values[2 * j] + c_im * values[2 * j + 1])
                acc_im = acc_im + (c_re * values[2 * j + 1] - c_im * values[2 * j])
            out_ref[2 * k, rows] = acc_re
            out_ref[2 * k + 1, rows] = acc_im
        return carry

    lax.fori_loop(0, chunks, combine, 0)


def orthogonalize(core, probe, mine, other, divisor):
    planes, width = probe.shape[0], probe.shape[-1]
    modes = planes // 2
    side = 16
    return pl.pallas_call(
        functools.partial(orthogonal_kernel, 1.0 / divisor),
        out_shape=shape(*probe.shape),
        in_specs=[SMEM, VMEM, ANY, ANY],
        out_specs=VMEM,
        scratch_shapes=[
            pltpu.VMEM(probe.shape, f32),
            pltpu.VMEM(probe.shape, f32),
            pltpu.VMEM((2, side, side, width), f32),
            pltpu.VMEM((2, side, width), f32),
            pltpu.VMEM((modes * (modes - 1), 8, width), f32),
            DMA((2,)),
        ],
        compiler_params=params(32),
        name="orthogonalize",
    )(core, probe, mine, other)


def moved(shard, axes, pairs):
    return lax.ppermute(shard, axes, pairs)


def shifted(size, by):
    return [(i, i + by) for i in range(size) if 0 <= i + by < size]


def sum_share(keep, groups):
    members = len(groups[0])
    parts = keep.reshape(members, -1, keep.shape[-1])
    parts = lax.all_to_all(parts, ("row", "col"), 0, 0, axis_index_groups=groups)
    return jnp.sum(parts, axis=0)


def gather_shares(share, groups):
    members = len(groups[0])
    parts = jnp.broadcast_to(share[None], (members,) + share.shape)
    return lax.all_to_all(parts, ("row", "col"), 0, 0, axis_index_groups=groups)


def local(object_slices, probe, measured, positions, counts):
    rows, cols = lax.axis_size("row"), lax.axis_size("col")
    modes, width = probe.shape[0], probe.shape[-1]
    planes = probe.reshape(2 * modes, width, width)
    capacity = positions.shape[2]
    spots = positions[:, 0]
    core = (lax.axis_index("row") % 2).astype(jnp.int32).reshape(1, 1)
    left_one, right_one = shifted(cols, -1), shifted(cols, 1)
    up_one, down_one = shifted(rows, -1), shifted(rows, 1)
    swap = [(r, r ^ 1) for r in range(rows)]
    groups = core_groups(rows, cols, 2)

    middle = object_slices.shape[2] // 2
    top = moved(object_slices[:, :, :middle, :width], "col", left_one)
    rest = moved(object_slices[:, :, middle:, :width], "col", left_one)
    below = [moved(object_slices[s : s + 1, :, :width, :], "row", up_one) for s in range(2)]
    corner = moved(top[:, :, :width], "row", up_one)
    keep, give, terms, right_top, right_rest, *below_grads, corner_grad = run_slots(
        counts, spots, core, object_slices, (top, rest, *below, corner), planes, measured[0]
    )
    keep = keep + moved(give, "row", swap)
    left_rest = moved(right_rest, "col", right_one)
    right_top = right_top.at[:, :, :width].add(moved(corner_grad, "row", down_one))
    left_top = moved(right_top, "col", right_one)
    above = [moved(part, "row", down_one) for part in below_grads]
    share = sum_share(keep, groups)
    mine = gather_shares(share, groups).reshape(keep.shape)
    object_next = settle(counts, spots, object_slices, terms, (left_top, left_rest), above)
    mine, object_next = lax.optimization_barrier((mine, object_next))
    other = moved(mine, "row", swap)
    divisor = math.sqrt(rows * cols * capacity)
    probe_next = orthogonalize(core, planes, mine, other, divisor).reshape(probe.shape)
    return (object_next, probe_next)


def solution(mesh):
    return jax.shard_map(
        local,
        mesh=mesh,
        in_specs=(
            P(None, None, "row", "col"),
            P(),
            P("row", "col", None, None),
            P(None, "row", "col"),
            P("row", "col"),
        ),
        out_specs=(P(None, None, "row", "col"), P()),
        check_vma=False,
    )
```

```python
import functools
import math

import jax
import jax.numpy as jnp
import numpy as np
from jax import lax
from jax.experimental import pallas as pl
from jax.experimental.pallas import tpu as pltpu
from jax.sharding import PartitionSpec as P

FRESNEL = 40.0
f32 = jnp.float32
bf16 = jnp.bfloat16


def complex_block(matrix):
    return np.block([[matrix.real, matrix.imag], [-matrix.imag, matrix.real]])


def split_table(block):
    block = block.astype(np.float32)
    high = block.astype(jnp.bfloat16)
    low = (block - high.astype(np.float32)).astype(jnp.bfloat16)
    return np.stack([high, low])


def make_tables(width):
    index = np.arange(width)
    fourier = np.exp(-2j * np.pi / width * (index[:, None] * index[None, :] % width)) / np.sqrt(width)
    frequency = np.where(index < width // 2, index, index - width) / width
    chirp = np.exp(-1j * FRESNEL * frequency**2)
    spread = fourier.conj() @ (chirp[:, None] * fourier)
    forward = complex_block(fourier)
    step = complex_block(spread)
    steps = np.stack([split_table(step), split_table(step.T)])
    transforms = np.stack([split_table(forward), split_table(forward.T)])
    return steps, transforms


def split(values):
    high = values.astype(bf16)
    low = (values - high.astype(f32)).astype(bf16)
    return high, low


def mm(left, right):
    return jnp.dot(left, right, preferred_element_type=f32)


def times_right(planes, table):
    a_re, a_im, b_re, b_im = planes
    stacked = jnp.concatenate(
        [jnp.concatenate([a_re, a_im], axis=1), jnp.concatenate([b_re, b_im], axis=1)], axis=0
    )
    high, low = split(stacked)
    out = mm(high, table[0]) + mm(low, table[0]) + mm(high, table[1])
    w = a_re.shape[0]
    return out[:w, :w], out[:w, w:], out[w:, :w], out[w:, w:]


def times_left(planes, table):
    a_re, a_im, b_re, b_im = planes
    stacked = jnp.concatenate(
        [jnp.concatenate([a_re, b_re], axis=1), jnp.concatenate([a_im, b_im], axis=1)], axis=0
    )
    high, low = split(stacked)
    out = mm(table[0], high) + mm(table[0], low) + mm(table[1], high)
    w = a_re.shape[0]
    return out[:w, :w], out[w:, :w], out[:w, w:], out[w:, w:]


def cmul(planes, re, im):
    a_re, a_im, b_re, b_im = planes
    return (
        a_re * re - a_im * im,
        a_re * im + a_im * re,
        b_re * re - b_im * im,
        b_re * im + b_im * re,
    )


def cmul_conj(planes, re, im):
    a_re, a_im, b_re, b_im = planes
    return (
        a_re * re + a_im * im,
        a_im * re - a_re * im,
        b_re * re + b_im * im,
        b_im * re - b_re * im,
    )


def overlap(wave, grad):
    re = wave[0] * grad[0] + wave[1] * grad[1] + wave[2] * grad[2] + wave[3] * grad[3]
    im = wave[0] * grad[1] - wave[1] * grad[0] + wave[2] * grad[3] - wave[3] * grad[2]
    return re, im


RIGHT, LEFT = 0, 1


def start_all(pairs, sems):
    copies = [pltpu.make_async_copy(src, dst, sems.at[i]) for i, (src, dst) in enumerate(pairs)]
    for copy in copies:
        copy.start()
    return copies


def near_sheet(tile, below, sheet, width):
    rows, cols = tile.shape[2:]
    down, across = pl.ds(rows, width), pl.ds(0, cols)
    return [(tile, sheet.at[:, :, pl.ds(0, rows), across])] + [
        (part, sheet.at[pl.ds(s, 1), :, down, across]) for s, part in enumerate(below)
    ]


def far_sheet(tile, right, below, corner, sheet, width):
    rows, cols = tile.shape[2:]
    down, across, last = pl.ds(rows, width), pl.ds(cols, width), pl.ds(cols - width, width)
    return (
        [(tile.at[:, :, :, last], sheet.at[:, :, pl.ds(0, rows), last])]
        + [(right, sheet.at[:, :, pl.ds(0, rows), across])]
        + [
            (part.at[:, :, :, last], sheet.at[pl.ds(s, 1), :, down, last])
            for s, part in enumerate(below)
        ]
        + [(corner, sheet.at[:, :, down, across])]
    )


def corner_of(pos_ref, slot, width):
    top = pos_ref[0, slot]
    left = pos_ref[1, slot]
    top8 = pl.multiple_of((top // 8) * 8, 8)
    left128 = pl.multiple_of((left // width) * width, width)
    return top8, left128, top - top8, left - left128


def cut_window(sheet, layer, plane, corner, width):
    top8, left128, drop_r, drop_c = corner
    wide = sheet[layer, plane, pl.ds(top8, width + 8), pl.ds(left128, 2 * width)]
    wide = pltpu.roll(wide, 2 * width - drop_c, 1)[:, :width]
    return pltpu.roll(wide, width + 8 - drop_r, 0)[:width]


def load4(ref, pair):
    return tuple(ref[pair * 4 + i] for i in range(4))


def store4(ref, pair, values):
    for i in range(4):
        ref[pair * 4 + i] = values[i]


def subtract_terms(slot, pos_ref, terms, sheet, width):
    top8, left128, drop_r, drop_c = corner_of(pos_ref, slot, width)
    for s in range(2):
        for c in range(2):
            wide = jnp.concatenate([terms[slot, s, c], jnp.zeros((8, width), f32)], axis=0)
            wide = pltpu.roll(wide, drop_r, 0)
            wide = jnp.concatenate([wide, jnp.zeros_like(wide)], axis=1)
            wide = pltpu.roll(wide, drop_c, 1)
            where = (s, c, pl.ds(top8, width + 8), pl.ds(left128, 2 * width))
            sheet[where] = sheet[where] - wide


def visit_slots(
    chosen, count, pos_ref, leaves, term_out, sheet, outer, probe, patterns, steps, transforms,
    window, wave, far, inten, pgrad, terms, sem_term,
):
    width = probe.shape[-1]
    pairs = probe.shape[0] // 4

    def save(slot):
        return pltpu.make_async_copy(terms.at[slot], term_out.at[slot], sem_term.at[slot])

    def process(slot):
        place = corner_of(pos_ref, slot, width)
        for s in range(2):
            for c in range(2):
                window[s, c] = cut_window(sheet, s, c, place, width)
        waves = [cmul(load4(probe, p), window[0, 0], window[0, 1]) for p in range(pairs)]
        waves = [times_right(v, steps[RIGHT]) for v in waves]
        waves = [times_left(v, steps[LEFT]) for v in waves]
        for p, v in enumerate(waves):
            store4(wave, p, v)
        waves = [cmul(v, window[1, 0], window[1, 1]) for v in waves]
        waves = [times_right(v, transforms[RIGHT]) for v in waves]
        waves = [times_left(v, transforms[LEFT]) for v in waves]
        total = -patterns[slot]
        for p, v in enumerate(waves):
            store4(far, p, v)
            total = total + (v[0] * v[0] + v[1] * v[1] + v[2] * v[2] + v[3] * v[3])
        inten[...] = total

        residual = inten[...]
        grads = [tuple(residual * x for x in load4(far, p)) for p in range(pairs)]
        grads = [times_right(v, transforms[LEFT]) for v in grads]
        grads = [times_left(v, transforms[RIGHT]) for v in grads]
        products = [overlap(load4(wave, p), v) for p, v in enumerate(grads)]
        terms[slot, 1, 0] = sum(t[0] for t in products)
        terms[slot, 1, 1] = sum(t[1] for t in products)
        grads = [cmul_conj(v, window[1, 0], window[1, 1]) for v in grads]
        grads = [times_right(v, steps[LEFT]) for v in grads]
        grads = [times_left(v, steps[RIGHT]) for v in grads]
        products = [overlap(load4(probe, p), v) for p, v in enumerate(grads)]
        terms[slot, 0, 0] = sum(t[0] for t in products)
        terms[slot, 0, 1] = sum(t[1] for t in products)
        grads = [cmul_conj(v, window[0, 0], window[0, 1]) for v in grads]
        for p, v in enumerate(grads):
            for i in range(4):
                pgrad[p * 4 + i] += v[i]
        save(slot).start()

        @pl.when(leaves(slot))
        def _():
            subtract_terms(slot, pos_ref, terms, outer, width)

    def visit(slot, carry):
        pl.when(chosen(slot))(lambda: process(slot))
        return carry

    def finish(slot, carry):
        pl.when(chosen(slot))(lambda: save(slot).wait())
        return carry

    lax.fori_loop(0, count, visit, 0)
    return lambda: lax.fori_loop(0, count, finish, 0)


def near_kernel(
    count_ref, pos_ref, tile, below_first, below_second, probe_in, pattern_in, step_in,
    transform_in,
    pgrad_out, term_out, below_out,
    sheet, outer, probe, patterns, steps, transforms, window, wave, far, inten, pgrad, terms,
    sem_in, sem_term, sem_out,
):
    width = probe.shape[-1]
    rows, cols = tile.shape[2:]
    loads = start_all(
        near_sheet(tile, (below_first, below_second), sheet, width)
        + [(probe_in, probe), (step_in, steps), (transform_in, transforms), (pattern_in, patterns)],
        sem_in,
    )
    outside = outer.at[:, :, pl.ds(rows, width), pl.ds(0, cols)]
    pgrad[...] = jnp.zeros_like(pgrad)
    outside[...] = jnp.zeros((2, 2, width, cols), f32)
    for copy in loads:
        copy.wait()
    wait_terms = visit_slots(
        lambda slot: pos_ref[1, slot] <= cols - width, count_ref[0, 0], pos_ref,
        lambda slot: pos_ref[0, slot] > rows - width,
        term_out, sheet, outer, probe, patterns, steps, transforms, window, wave, far, inten,
        pgrad, terms, sem_term,
    )
    stores = start_all([(pgrad, pgrad_out), (outside, below_out)], sem_out)
    wait_terms()
    for copy in stores:
        copy.wait()


def far_kernel(
    count_ref, pos_ref, core_ref, tile, right, below_first, below_second, corner, probe_in,
    pattern_in, step_in, transform_in, pgrad_in, below_in, term_in,
    keep_out, give_out, right_top_out, right_rest_out, below_first_out, below_second_out,
    corner_out, term_out,
    sheet, outer, probe, patterns, steps, transforms, window, wave, far, inten, pgrad, terms,
    sem_in, sem_term, sem_out,
):
    width = probe.shape[-1]
    planes = probe.shape[0]
    rows, cols = tile.shape[2:]
    down, across, inner = pl.ds(rows, width), pl.ds(cols, width), pl.ds(0, cols)
    loads = start_all(
        far_sheet(tile, right, (below_first, below_second), corner, sheet, width)
        + [(probe_in, probe), (step_in, steps), (transform_in, transforms), (pattern_in, patterns)]
        + [(pgrad_in, pgrad), (below_in, outer.at[:, :, down, inner])],
        sem_in,
    )
    outer[:, :, 0 : rows + width, cols : cols + width] = jnp.zeros((2, 2, rows + width, width), f32)
    for copy in loads:
        copy.wait()
    wait_terms = visit_slots(
        lambda slot: pos_ref[1, slot] > cols - width, count_ref[0, 0], pos_ref,
        lambda slot: pos_ref[1, slot] > cols - width,
        term_out, sheet, outer, probe, patterns, steps, transforms, window, wave, far, inten,
        pgrad, terms, sem_term,
    )
    half = planes // 2
    core = core_ref[0, 0]
    stores = start_all(
        [
            (pgrad.at[pl.ds((1 - core) * half, half)], give_out),
            (pgrad.at[pl.ds(core * half, half)], keep_out),
            (outer.at[:, :, down, across], corner_out),
            (outer.at[:, :, pl.ds(width, rows - width), across], right_rest_out),
            (outer.at[:, :, pl.ds(0, width), across], right_top_out),
            (outer.at[pl.ds(0, 1), :, down, inner], below_first_out),
            (outer.at[pl.ds(1, 1), :, down, inner], below_second_out),
        ],
        sem_out,
    )
    wait_terms()
    for copy in stores:
        copy.wait()


def load_terms(count, term_in, terms, sems):
    def fetch(slot):
        return pltpu.make_async_copy(term_in.at[slot], terms.at[slot], sems.at[slot])

    def begin(slot, carry):
        fetch(slot).start()
        return carry

    def finish(slot, carry):
        fetch(slot).wait()
        return carry

    lax.fori_loop(0, count, begin, 0)
    return lambda: lax.fori_loop(0, count, finish, 0)


def settle_kernel(
    count_ref, pos_ref, tile, term_in, left_top_in, left_rest_in, above_first_in, above_second_in, corner_in,
    tile_out,
    sheet, terms, left, above, corner, sem_term, sem_in, sem_out,
):
    width = above_first_in.shape[2]
    rows, cols = tile.shape[2:]
    count = count_ref[0, 0]
    inner = sheet.at[:, :, pl.ds(0, rows), pl.ds(0, cols)]
    sources = [
        (tile, inner),
        (left_top_in, left.at[:, :, pl.ds(0, width)]),
        (left_rest_in, left.at[:, :, pl.ds(width, rows - width)]),
        (above_first_in, above.at[pl.ds(0, 1)]),
        (above_second_in, above.at[pl.ds(1, 1)]),
        (corner_in, corner),
    ]
    loads = [
        pltpu.make_async_copy(src, dst, sem_in.at[i]) for i, (src, dst) in enumerate(sources)
    ]
    for copy in loads:
        copy.start()
    wait = load_terms(count, term_in, terms, sem_term)
    for copy in loads:
        copy.wait()
    wait()
    sheet[:, :, 0:rows, 0:width] += left[...]
    sheet[:, :, 0:width, 0:cols] += above[...]
    sheet[:, :, 0:width, 0:width] += corner[...]

    def visit(slot, carry):
        subtract_terms(slot, pos_ref, terms, sheet, width)
        return carry

    lax.fori_loop(0, count, visit, 0)
    store = pltpu.make_async_copy(inner, tile_out, sem_out.at[0])
    store.start()
    store.wait()


VMEM = pl.BlockSpec(memory_space=pltpu.VMEM)
SMEM = pl.BlockSpec(memory_space=pltpu.SMEM)
ANY = pl.BlockSpec(memory_space=pl.ANY)
DMA = pltpu.SemaphoreType.DMA


def shape(*dims):
    return jax.ShapeDtypeStruct(dims, f32)


def params(mib):
    return pltpu.CompilerParams(vmem_limit_bytes=mib * 1024 * 1024)


def work(products):
    return pl.CostEstimate(
        flops=products * 2 * 256**3, bytes_accessed=8 * 1024 * 1024, transcendentals=0
    )


def slot_scratch(rows, cols, capacity, probe, steps, transforms, loads, stores):
    width = probe.shape[-1]
    stack = pltpu.VMEM(probe.shape, f32)
    field = pltpu.VMEM((2, 2, rows + width + 8, cols + 2 * width), f32)
    return [
        field,
        field,
        stack,
        pltpu.VMEM((capacity, width, width), f32),
        pltpu.VMEM(steps.shape, bf16),
        pltpu.VMEM(transforms.shape, bf16),
        pltpu.VMEM((2, 2, width, width), f32),
        stack,
        stack,
        pltpu.VMEM((width, width), f32),
        stack,
        pltpu.VMEM((capacity, 2, 2, width, width), f32),
        DMA((loads,)),
        DMA((capacity,)),
        DMA((stores,)),
    ]


def near_slots(counts, positions, tile, below, probe, patterns, tables, products):
    width = probe.shape[-1]
    rows, cols = tile.shape[2:]
    capacity = positions.shape[1]
    return pl.pallas_call(
        near_kernel,
        out_shape=[
            shape(*probe.shape),
            shape(capacity, 2, 2, width, width),
            shape(2, 2, width, cols),
        ],
        in_specs=[SMEM, SMEM] + [ANY] * 7,
        out_specs=[ANY] * 3,
        scratch_shapes=slot_scratch(rows, cols, capacity, probe, *tables, 7, 2),
        compiler_params=params(60),
        cost_estimate=work(products),
        name="near_slots",
    )(counts, positions, tile, *below, probe, patterns, *tables)


def far_slots(counts, positions, core, tile, halo, probe, patterns, tables, sums):
    planes, width = probe.shape[0], probe.shape[-1]
    rows, cols = tile.shape[2:]
    capacity = positions.shape[1]
    half = shape(planes // 2, width, width)
    return pl.pallas_call(
        far_kernel,
        out_shape=[
            half,
            half,
            shape(2, 2, width, width),
            shape(2, 2, rows - width, width),
            shape(1, 2, width, cols),
            shape(1, 2, width, cols),
            shape(2, 2, width, width),
            shape(capacity, 2, 2, width, width),
        ],
        in_specs=[SMEM, SMEM, SMEM] + [ANY] * 12,
        out_specs=[ANY] * 8,
        scratch_shapes=slot_scratch(rows, cols, capacity, probe, *tables, 11, 7),
        input_output_aliases={14: 7},
        compiler_params=params(60),
        cost_estimate=work(4 * capacity * planes),
        name="far_slots",
    )(counts, positions, core, tile, *halo, probe, patterns, *tables, *sums)


def settle(counts, positions, tile, terms, left, above, corner):
    capacity, width = terms.shape[0], terms.shape[-1]
    rows, cols = tile.shape[2:]
    return pl.pallas_call(
        settle_kernel,
        out_shape=shape(*tile.shape),
        in_specs=[SMEM, SMEM] + [ANY] * 7,
        out_specs=ANY,
        scratch_shapes=[
            pltpu.VMEM((2, 2, rows + width + 8, cols + 2 * width), f32),
            pltpu.VMEM(terms.shape, f32),
            pltpu.VMEM((2, 2, rows, width), f32),
            pltpu.VMEM((2, 2, width, cols), f32),
            pltpu.VMEM(corner.shape, f32),
            DMA((capacity,)),
            DMA((6,)),
            DMA((1,)),
        ],
        compiler_params=params(60),
        cost_estimate=work(4096),
        name="settle",
    )(counts, positions, tile, terms, *left, *above, corner)


def core_groups(rows, cols, split):
    return [
        [r * cols + c for r in range(part, rows, split) for c in range(cols)]
        for part in range(split)
    ]


def orthogonal_kernel(
    scale, core_ref, probe_ref, mine, other, out_ref, total, stepped, sums, gram, coef, sem
):
    planes, width = probe_ref.shape[0], probe_ref.shape[-1]
    half = planes // 2
    core = core_ref[0, 0]
    loads = [
        pltpu.make_async_copy(mine, total.at[pl.ds(core * half, half)], sem.at[0]),
        pltpu.make_async_copy(other, total.at[pl.ds((1 - core) * half, half)], sem.at[1]),
    ]
    for copy in loads:
        copy.start()
    for copy in loads:
        copy.wait()
    modes = planes // 2
    sub = 8
    chunks = width // sub
    stepped[...] = probe_ref[...] - total[...] * scale

    block = 3
    sums[...] = jnp.zeros_like(sums)
    for jb in range(0, modes, block):
        for kb in range(jb, modes, block):
            pairs = [
                (j, k) for j in range(jb, jb + block) for k in range(kb, kb + block) if j <= k
            ]

            def accumulate(chunk, carried):
                rows = pl.ds(pl.multiple_of(chunk * sub, sub), sub)
                left = {j: (stepped[2 * j, rows], stepped[2 * j + 1, rows]) for j in range(jb, jb + block)}
                right = {k: (stepped[2 * k, rows], stepped[2 * k + 1, rows]) for k in range(kb, kb + block)}
                out = []
                for (j, k), (acc_re, acc_im) in zip(pairs, carried):
                    (l_re, l_im), (r_re, r_im) = left[j], right[k]
                    out.append(
                        (
                            acc_re + l_re * r_re + l_im * r_im,
                            acc_im + l_re * r_im - l_im * r_re,
                        )
                    )
                return out

            zero = jnp.zeros((sub, width), f32)
            result = lax.fori_loop(
                0, chunks, accumulate, [(zero, zero) for _ in pairs], unroll=4
            )
            for (j, k), (acc_re, acc_im) in zip(pairs, result):
                s_re = jnp.sum(acc_re, axis=0, keepdims=True)
                s_im = jnp.sum(acc_im, axis=0, keepdims=True)
                sums[0, j, k : k + 1] = s_re
                sums[1, j, k : k + 1] = s_im
                if j != k:
                    sums[0, k, j : j + 1] = s_re
                    sums[1, k, j : j + 1] = -s_im
    side = sums.shape[1]
    ones = jnp.ones((sub, width), f32)
    for part in range(2):
        for j in range(modes):
            row = lax.dot_general(
                ones, sums[part, j], (((1,), (1,)), ((), ())),
                precision=lax.Precision.HIGHEST, preferred_element_type=f32,
            )
            gram[part, j : j + 1, 0:side] = row[0:1]

    row_id = lax.broadcasted_iota(jnp.int32, (side, width), 0)
    lane_id = lax.broadcasted_iota(jnp.int32, (side, width), 1)
    valid = (row_id < modes) & (lane_id < modes)
    eye = jnp.where((lane_id == row_id + side) & (row_id < modes), 1.0, 0.0)
    work_re = jnp.where(valid, gram[0], 0.0) + eye
    work_im = jnp.where(valid, gram[1], 0.0)
    for k in range(modes - 1):
        row_re = work_re[k : k + 1]
        row_im = work_im[k : k + 1]
        inverse = 1.0 / work_re[k : k + 1, k : k + 1]
        f_re = jnp.where(row_id[:, :1] > k, work_re[:, k : k + 1] * inverse, 0.0)
        f_im = jnp.where(row_id[:, :1] > k, work_im[:, k : k + 1] * inverse, 0.0)
        work_re, work_im = (
            work_re - (f_re * row_re - f_im * row_im),
            work_im - (f_re * row_im + f_im * row_re),
        )
    place = 0
    for k in range(modes):
        for j in range(k):
            coef[place] = jnp.broadcast_to(work_re[k : k + 1, side + j : side + j + 1], (sub, width))
            coef[place + 1] = jnp.broadcast_to(work_im[k : k + 1, side + j : side + j + 1], (sub, width))
            place += 2

    def combine(chunk, carry):
        rows = pl.ds(pl.multiple_of(chunk * sub, sub), sub)
        values = [stepped[i, rows] for i in range(planes)]
        place = 0
        for k in range(modes):
            acc_re, acc_im = values[2 * k], values[2 * k + 1]
            for j in range(k):
                c_re, c_im = coef[place], coef[place + 1]
                place += 2
                acc_re = acc_re + (c_re * values[2 * j] + c_im * values[2 * j + 1])
                acc_im = acc_im + (c_re * values[2 * j + 1] - c_im * values[2 * j])
            out_ref[2 * k, rows] = acc_re
            out_ref[2 * k + 1, rows] = acc_im
        return carry

    lax.fori_loop(0, chunks, combine, 0)


def orthogonalize(core, probe, mine, other, divisor):
    planes, width = probe.shape[0], probe.shape[-1]
    modes = planes // 2
    side = 16
    return pl.pallas_call(
        functools.partial(orthogonal_kernel, 1.0 / divisor),
        out_shape=shape(*probe.shape),
        in_specs=[SMEM, VMEM, ANY, ANY],
        out_specs=VMEM,
        scratch_shapes=[
            pltpu.VMEM(probe.shape, f32),
            pltpu.VMEM(probe.shape, f32),
            pltpu.VMEM((2, side, side, width), f32),
            pltpu.VMEM((2, side, width), f32),
            pltpu.VMEM((modes * (modes - 1), 8, width), f32),
            DMA((2,)),
        ],
        compiler_params=params(32),
        name="orthogonalize",
    )(core, probe, mine, other)


def moved(shard, axes, pairs):
    return lax.ppermute(shard, axes, pairs)


def shifted(size, by):
    return [(i, i + by) for i in range(size) if 0 <= i + by < size]


def shifted_both(rows, cols, by):
    return [
        (r * cols + c, (r + by) * cols + c + by)
        for r in range(rows)
        for c in range(cols)
        if 0 <= r + by < rows and 0 <= c + by < cols
    ]


def sum_share(keep, groups):
    members = len(groups[0])
    parts = keep.reshape(members, -1, keep.shape[-1])
    parts = lax.all_to_all(parts, ("row", "col"), 0, 0, axis_index_groups=groups)
    return jnp.sum(parts, axis=0)


def gather_shares(share, groups):
    members = len(groups[0])
    parts = jnp.broadcast_to(share[None], (members,) + share.shape)
    return lax.all_to_all(parts, ("row", "col"), 0, 0, axis_index_groups=groups)


def local(object_slices, probe, measured, positions, counts):
    rows, cols = lax.axis_size("row"), lax.axis_size("col")
    modes, width = probe.shape[0], probe.shape[-1]
    planes = probe.reshape(2 * modes, width, width)
    capacity = positions.shape[2]
    spots = positions[:, 0]
    core = (lax.axis_index("row") % 2).astype(jnp.int32).reshape(1, 1)
    left_one, right_one = shifted(cols, -1), shifted(cols, 1)
    up_one, down_one = shifted(rows, -1), shifted(rows, 1)
    swap = [(r, r ^ 1) for r in range(rows)]
    groups = core_groups(rows, cols, 2)

    right = moved(object_slices[:, :, :, :width], "col", left_one)
    below = [moved(object_slices[s : s + 1, :, :width, :], "row", up_one) for s in range(2)]
    corner = moved(object_slices[:, :, :width, :width], ("row", "col"), shifted_both(rows, cols, -1))
    tables = [jnp.asarray(t) for t in make_tables(width)]
    probe_sum, terms, below_sum = near_slots(
        counts, spots, object_slices, below, planes, measured[0], tables, 1
    )
    keep, give, right_top, right_rest, *below_grads, corner_grad, terms = far_slots(
        counts, spots, core, object_slices, (right, *below, corner), planes, measured[0],
        tables, (probe_sum, below_sum, terms),
    )
    keep = keep + moved(give, "row", swap)
    left_rest = moved(right_rest, "col", right_one)
    from_corner = moved(corner_grad, ("row", "col"), shifted_both(rows, cols, 1))
    left_top = moved(right_top, "col", right_one)
    above = [moved(part, "row", down_one) for part in below_grads]
    share = sum_share(keep, groups)
    mine = gather_shares(share, groups).reshape(keep.shape)
    object_next = settle(counts, spots, object_slices, terms, (left_top, left_rest), above, from_corner)
    mine, object_next = lax.optimization_barrier((mine, object_next))
    other = moved(mine, "row", swap)
    divisor = math.sqrt(rows * cols * capacity)
    probe_next = orthogonalize(core, planes, mine, other, divisor).reshape(probe.shape)
    return (object_next, probe_next)


def solution(mesh):
    return jax.shard_map(
        local,
        mesh=mesh,
        in_specs=(
            P(None, None, "row", "col"),
            P(),
            P("row", "col", None, None),
            P(None, "row", "col"),
            P("row", "col"),
        ),
        out_specs=(P(None, None, "row", "col"), P()),
        check_vma=False,
    )
```

```python
import functools
import math

import jax
import jax.numpy as jnp
import numpy as np
from jax import lax
from jax.experimental import pallas as pl
from jax.experimental.pallas import tpu as pltpu
from jax.sharding import PartitionSpec as P

FRESNEL = 40.0
f32 = jnp.float32
bf16 = jnp.bfloat16


def complex_block(matrix):
    return np.block([[matrix.real, matrix.imag], [-matrix.imag, matrix.real]])


def split_table(block):
    block = block.astype(np.float32)
    high = block.astype(jnp.bfloat16)
    low = (block - high.astype(np.float32)).astype(jnp.bfloat16)
    return np.stack([high, low])


def make_tables(width):
    index = np.arange(width)
    fourier = np.exp(-2j * np.pi / width * (index[:, None] * index[None, :] % width)) / np.sqrt(width)
    frequency = np.where(index < width // 2, index, index - width) / width
    chirp = np.exp(-1j * FRESNEL * frequency**2)
    spread = fourier.conj() @ (chirp[:, None] * fourier)
    forward = complex_block(fourier)
    step = complex_block(spread)
    steps = np.stack([split_table(step), split_table(step.T)])
    transforms = np.stack([split_table(forward), split_table(forward.T)])
    return steps, transforms


def split(values):
    high = values.astype(bf16)
    low = (values - high.astype(f32)).astype(bf16)
    return high, low


def mm(left, right):
    return jnp.dot(left, right, preferred_element_type=f32)


def times_right(planes, table):
    a_re, a_im, b_re, b_im = planes
    stacked = jnp.concatenate(
        [jnp.concatenate([a_re, a_im], axis=1), jnp.concatenate([b_re, b_im], axis=1)], axis=0
    )
    high, low = split(stacked)
    out = mm(high, table[0]) + mm(low, table[0]) + mm(high, table[1])
    w = a_re.shape[0]
    return out[:w, :w], out[:w, w:], out[w:, :w], out[w:, w:]


def times_left(planes, table):
    a_re, a_im, b_re, b_im = planes
    stacked = jnp.concatenate(
        [jnp.concatenate([a_re, b_re], axis=1), jnp.concatenate([a_im, b_im], axis=1)], axis=0
    )
    high, low = split(stacked)
    both = mm(jnp.concatenate([table[0], table[1]], axis=0), high)
    side = stacked.shape[0]
    out = both[:side] + both[side:] + mm(table[0], low)
    w = a_re.shape[0]
    return out[:w, :w], out[w:, :w], out[:w, w:], out[w:, w:]


def cmul(planes, re, im):
    a_re, a_im, b_re, b_im = planes
    return (
        a_re * re - a_im * im,
        a_re * im + a_im * re,
        b_re * re - b_im * im,
        b_re * im + b_im * re,
    )


def cmul_conj(planes, re, im):
    a_re, a_im, b_re, b_im = planes
    return (
        a_re * re + a_im * im,
        a_im * re - a_re * im,
        b_re * re + b_im * im,
        b_im * re - b_re * im,
    )


def overlap(wave, grad):
    re = wave[0] * grad[0] + wave[1] * grad[1] + wave[2] * grad[2] + wave[3] * grad[3]
    im = wave[0] * grad[1] - wave[1] * grad[0] + wave[2] * grad[3] - wave[3] * grad[2]
    return re, im


RIGHT, LEFT = 0, 1


def start_all(pairs, sems):
    copies = [pltpu.make_async_copy(src, dst, sems.at[i]) for i, (src, dst) in enumerate(pairs)]
    for copy in copies:
        copy.start()
    return copies


def near_sheet(tile, below, sheet, width):
    rows, cols = tile.shape[2:]
    down, across = pl.ds(rows, width), pl.ds(0, cols)
    return [(tile, sheet.at[:, :, pl.ds(0, rows), across])] + [
        (part, sheet.at[pl.ds(s, 1), :, down, across]) for s, part in enumerate(below)
    ]


def far_sheet(tile, right, below, corner, sheet, width):
    rows, cols = tile.shape[2:]
    down, across, last = pl.ds(rows, width), pl.ds(cols, width), pl.ds(cols - width, width)
    return (
        [(tile.at[:, :, :, last], sheet.at[:, :, pl.ds(0, rows), last])]
        + [(part, sheet.at[:, :, pl.ds(r, part.shape[2]), across]) for r, part in right]
        + [
            (part.at[:, :, :, last], sheet.at[pl.ds(s, 1), :, down, last])
            for s, part in enumerate(below)
        ]
        + [(corner, sheet.at[:, :, down, across])]
    )


def corner_of(pos_ref, slot, width):
    top = pos_ref[0, slot]
    left = pos_ref[1, slot]
    top8 = pl.multiple_of((top // 8) * 8, 8)
    left128 = pl.multiple_of((left // width) * width, width)
    return top8, left128, top - top8, left - left128


def cut_window(sheet, layer, plane, corner, width):
    top8, left128, drop_r, drop_c = corner
    wide = sheet[layer, plane, pl.ds(top8, width + 8), pl.ds(left128, 2 * width)]
    wide = pltpu.roll(wide, 2 * width - drop_c, 1)[:, :width]
    return pltpu.roll(wide, width + 8 - drop_r, 0)[:width]


def load4(ref, pair):
    return tuple(ref[pair * 4 + i] for i in range(4))


def store4(ref, pair, values):
    for i in range(4):
        ref[pair * 4 + i] = values[i]


def subtract_terms(slot, pos_ref, terms, sheet, width):
    top8, left128, drop_r, drop_c = corner_of(pos_ref, slot, width)
    for s in range(2):
        for c in range(2):
            wide = jnp.concatenate([terms[slot, s, c], jnp.zeros((8, width), f32)], axis=0)
            wide = pltpu.roll(wide, drop_r, 0)
            wide = jnp.concatenate([wide, jnp.zeros_like(wide)], axis=1)
            wide = pltpu.roll(wide, drop_c, 1)
            where = (s, c, pl.ds(top8, width + 8), pl.ds(left128, 2 * width))
            sheet[where] = sheet[where] - wide


def visit_slots(
    chosen, count, pos_ref, leaves, term_out, sheet, outer, probe, patterns, steps, transforms,
    window, wave, far, inten, pgrad, terms, sem_term,
):
    width = probe.shape[-1]
    pairs = probe.shape[0] // 4

    def save(slot):
        return pltpu.make_async_copy(terms.at[slot], term_out.at[slot], sem_term.at[slot])

    def process(slot):
        place = corner_of(pos_ref, slot, width)
        for s in range(2):
            for c in range(2):
                window[s, c] = cut_window(sheet, s, c, place, width)
        waves = [cmul(load4(probe, p), window[0, 0], window[0, 1]) for p in range(pairs)]
        waves = [times_right(v, steps[RIGHT]) for v in waves]
        waves = [times_left(v, steps[LEFT]) for v in waves]
        for p, v in enumerate(waves):
            store4(wave, p, v)
        waves = [cmul(v, window[1, 0], window[1, 1]) for v in waves]
        waves = [times_right(v, transforms[RIGHT]) for v in waves]
        waves = [times_left(v, transforms[LEFT]) for v in waves]
        total = -patterns[slot]
        for p, v in enumerate(waves):
            store4(far, p, v)
            total = total + (v[0] * v[0] + v[1] * v[1] + v[2] * v[2] + v[3] * v[3])
        inten[...] = total

        residual = inten[...]
        grads = [tuple(residual * x for x in load4(far, p)) for p in range(pairs)]
        grads = [times_right(v, transforms[LEFT]) for v in grads]
        grads = [times_left(v, transforms[RIGHT]) for v in grads]
        products = [overlap(load4(wave, p), v) for p, v in enumerate(grads)]
        terms[slot, 1, 0] = sum(t[0] for t in products)
        terms[slot, 1, 1] = sum(t[1] for t in products)
        grads = [cmul_conj(v, window[1, 0], window[1, 1]) for v in grads]
        grads = [times_right(v, steps[LEFT]) for v in grads]
        grads = [times_left(v, steps[RIGHT]) for v in grads]
        products = [overlap(load4(probe, p), v) for p, v in enumerate(grads)]
        terms[slot, 0, 0] = sum(t[0] for t in products)
        terms[slot, 0, 1] = sum(t[1] for t in products)
        grads = [cmul_conj(v, window[0, 0], window[0, 1]) for v in grads]
        for p, v in enumerate(grads):
            for i in range(4):
                pgrad[p * 4 + i] += v[i]
        save(slot).start()

        @pl.when(leaves(slot))
        def _():
            subtract_terms(slot, pos_ref, terms, outer, width)

    def visit(slot, carry):
        pl.when(chosen(slot))(lambda: process(slot))
        return carry

    def finish(slot, carry):
        pl.when(chosen(slot))(lambda: save(slot).wait())
        return carry

    lax.fori_loop(0, count, visit, 0)
    return lambda: lax.fori_loop(0, count, finish, 0)


def near_kernel(
    count_ref, pos_ref, tile, below_first, below_second, probe_in, pattern_in, step_in,
    transform_in,
    pgrad_out, term_out, below_out,
    sheet, outer, probe, patterns, steps, transforms, window, wave, far, inten, pgrad, terms,
    sem_in, sem_term, sem_out,
):
    width = probe.shape[-1]
    rows, cols = tile.shape[2:]
    loads = start_all(
        near_sheet(tile, (below_first, below_second), sheet, width)
        + [(probe_in, probe), (step_in, steps), (transform_in, transforms), (pattern_in, patterns)],
        sem_in,
    )
    outside = outer.at[:, :, pl.ds(rows, width), pl.ds(0, cols)]
    pgrad[...] = jnp.zeros_like(pgrad)
    outside[...] = jnp.zeros((2, 2, width, cols), f32)
    for copy in loads:
        copy.wait()
    wait_terms = visit_slots(
        lambda slot: pos_ref[1, slot] <= cols - width, count_ref[0, 0], pos_ref,
        lambda slot: pos_ref[0, slot] > rows - width,
        term_out, sheet, outer, probe, patterns, steps, transforms, window, wave, far, inten,
        pgrad, terms, sem_term,
    )
    stores = start_all([(pgrad, pgrad_out), (outside, below_out)], sem_out)
    wait_terms()
    for copy in stores:
        copy.wait()


def far_kernel(
    count_ref, pos_ref, core_ref, tile, top, middle, bottom, below_first, below_second, corner, probe_in,
    pattern_in, step_in, transform_in, pgrad_in, below_in, term_in,
    keep_out, give_out, right_top_out, right_rest_out, below_first_out, below_second_out,
    corner_out, term_out,
    sheet, outer, probe, patterns, steps, transforms, window, wave, far, inten, pgrad, terms,
    sem_in, sem_term, sem_out,
):
    width = probe.shape[-1]
    planes = probe.shape[0]
    rows, cols = tile.shape[2:]
    down, across, inner = pl.ds(rows, width), pl.ds(cols, width), pl.ds(0, cols)
    right = [(0, top), (top.shape[2], middle), (rows - bottom.shape[2], bottom)]
    loads = start_all(
        far_sheet(tile, right, (below_first, below_second), corner, sheet, width)
        + [(probe_in, probe), (step_in, steps), (transform_in, transforms), (pattern_in, patterns)]
        + [(pgrad_in, pgrad), (below_in, outer.at[:, :, down, inner])],
        sem_in,
    )
    outer[:, :, 0 : rows + width, cols : cols + width] = jnp.zeros((2, 2, rows + width, width), f32)
    for copy in loads:
        copy.wait()
    wait_terms = visit_slots(
        lambda slot: pos_ref[1, slot] > cols - width, count_ref[0, 0], pos_ref,
        lambda slot: pos_ref[1, slot] > cols - width,
        term_out, sheet, outer, probe, patterns, steps, transforms, window, wave, far, inten,
        pgrad, terms, sem_term,
    )
    half = planes // 2
    core = core_ref[0, 0]
    stores = start_all(
        [
            (pgrad.at[pl.ds((1 - core) * half, half)], give_out),
            (pgrad.at[pl.ds(core * half, half)], keep_out),
            (outer.at[:, :, down, across], corner_out),
            (outer.at[:, :, pl.ds(width, rows - width), across], right_rest_out),
            (outer.at[:, :, pl.ds(0, width), across], right_top_out),
            (outer.at[pl.ds(0, 1), :, down, inner], below_first_out),
            (outer.at[pl.ds(1, 1), :, down, inner], below_second_out),
        ],
        sem_out,
    )
    wait_terms()
    for copy in stores:
        copy.wait()


def load_terms(count, term_in, terms, sems):
    def fetch(slot):
        return pltpu.make_async_copy(term_in.at[slot], terms.at[slot], sems.at[slot])

    def begin(slot, carry):
        fetch(slot).start()
        return carry

    def finish(slot, carry):
        fetch(slot).wait()
        return carry

    lax.fori_loop(0, count, begin, 0)
    return lambda: lax.fori_loop(0, count, finish, 0)


def settle_kernel(
    count_ref, pos_ref, tile, term_in, left_top_in, left_rest_in, above_first_in, above_second_in, corner_in,
    tile_out,
    sheet, terms, left, above, corner, sem_term, sem_in, sem_out,
):
    width = above_first_in.shape[2]
    rows, cols = tile.shape[2:]
    count = count_ref[0, 0]
    inner = sheet.at[:, :, pl.ds(0, rows), pl.ds(0, cols)]
    sources = [
        (tile, inner),
        (left_top_in, left.at[:, :, pl.ds(0, width)]),
        (left_rest_in, left.at[:, :, pl.ds(width, rows - width)]),
        (above_first_in, above.at[pl.ds(0, 1)]),
        (above_second_in, above.at[pl.ds(1, 1)]),
        (corner_in, corner),
    ]
    loads = [
        pltpu.make_async_copy(src, dst, sem_in.at[i]) for i, (src, dst) in enumerate(sources)
    ]
    for copy in loads:
        copy.start()
    wait = load_terms(count, term_in, terms, sem_term)
    for copy in loads:
        copy.wait()
    wait()
    sheet[:, :, 0:rows, 0:width] += left[...]
    sheet[:, :, 0:width, 0:cols] += above[...]
    sheet[:, :, 0:width, 0:width] += corner[...]

    def visit(slot, carry):
        subtract_terms(slot, pos_ref, terms, sheet, width)
        return carry

    lax.fori_loop(0, count, visit, 0)
    store = pltpu.make_async_copy(inner, tile_out, sem_out.at[0])
    store.start()
    store.wait()


VMEM = pl.BlockSpec(memory_space=pltpu.VMEM)
SMEM = pl.BlockSpec(memory_space=pltpu.SMEM)
ANY = pl.BlockSpec(memory_space=pl.ANY)
DMA = pltpu.SemaphoreType.DMA


def shape(*dims):
    return jax.ShapeDtypeStruct(dims, f32)


def params(mib):
    return pltpu.CompilerParams(vmem_limit_bytes=mib * 1024 * 1024)


def work(products):
    return pl.CostEstimate(
        flops=products * 2 * 256**3, bytes_accessed=8 * 1024 * 1024, transcendentals=0
    )


def slot_scratch(rows, cols, capacity, probe, steps, transforms, loads, stores):
    width = probe.shape[-1]
    stack = pltpu.VMEM(probe.shape, f32)
    field = pltpu.VMEM((2, 2, rows + width + 8, cols + 2 * width), f32)
    return [
        field,
        field,
        stack,
        pltpu.VMEM((capacity, width, width), f32),
        pltpu.VMEM(steps.shape, bf16),
        pltpu.VMEM(transforms.shape, bf16),
        pltpu.VMEM((2, 2, width, width), f32),
        stack,
        stack,
        pltpu.VMEM((width, width), f32),
        stack,
        pltpu.VMEM((capacity, 2, 2, width, width), f32),
        DMA((loads,)),
        DMA((capacity,)),
        DMA((stores,)),
    ]


def near_slots(counts, positions, tile, below, probe, patterns, tables, products):
    width = probe.shape[-1]
    rows, cols = tile.shape[2:]
    capacity = positions.shape[1]
    return pl.pallas_call(
        near_kernel,
        out_shape=[
            shape(*probe.shape),
            shape(capacity, 2, 2, width, width),
            shape(2, 2, width, cols),
        ],
        in_specs=[SMEM, SMEM] + [ANY] * 7,
        out_specs=[ANY] * 3,
        scratch_shapes=slot_scratch(rows, cols, capacity, probe, *tables, 7, 2),
        compiler_params=params(60),
        cost_estimate=work(products),
        name="near_slots",
    )(counts, positions, tile, *below, probe, patterns, *tables)


def far_slots(counts, positions, core, tile, halo, probe, patterns, tables, sums):
    planes, width = probe.shape[0], probe.shape[-1]
    rows, cols = tile.shape[2:]
    capacity = positions.shape[1]
    half = shape(planes // 2, width, width)
    return pl.pallas_call(
        far_kernel,
        out_shape=[
            half,
            half,
            shape(2, 2, width, width),
            shape(2, 2, rows - width, width),
            shape(1, 2, width, cols),
            shape(1, 2, width, cols),
            shape(2, 2, width, width),
            shape(capacity, 2, 2, width, width),
        ],
        in_specs=[SMEM, SMEM, SMEM] + [ANY] * 14,
        out_specs=[ANY] * 8,
        scratch_shapes=slot_scratch(rows, cols, capacity, probe, *tables, 13, 7),
        input_output_aliases={16: 7},
        compiler_params=params(60),
        cost_estimate=work(4 * capacity * planes),
        name="far_slots",
    )(counts, positions, core, tile, *halo, probe, patterns, *tables, *sums)


def settle(counts, positions, tile, terms, left, above, corner):
    capacity, width = terms.shape[0], terms.shape[-1]
    rows, cols = tile.shape[2:]
    return pl.pallas_call(
        settle_kernel,
        out_shape=shape(*tile.shape),
        in_specs=[SMEM, SMEM] + [ANY] * 7,
        out_specs=ANY,
        scratch_shapes=[
            pltpu.VMEM((2, 2, rows + width + 8, cols + 2 * width), f32),
            pltpu.VMEM(terms.shape, f32),
            pltpu.VMEM((2, 2, rows, width), f32),
            pltpu.VMEM((2, 2, width, cols), f32),
            pltpu.VMEM(corner.shape, f32),
            DMA((capacity,)),
            DMA((6,)),
            DMA((1,)),
        ],
        compiler_params=params(60),
        cost_estimate=work(4096),
        name="settle",
    )(counts, positions, tile, terms, *left, *above, corner)


def core_groups(rows, cols, split):
    return [
        [r * cols + c for r in range(part, rows, split) for c in range(cols)]
        for part in range(split)
    ]


def orthogonal_kernel(
    scale, core_ref, probe_ref, mine, other, out_ref, total, stepped, sums, gram, coef, sem
):
    planes, width = probe_ref.shape[0], probe_ref.shape[-1]
    half = planes // 2
    core = core_ref[0, 0]
    loads = [
        pltpu.make_async_copy(mine, total.at[pl.ds(core * half, half)], sem.at[0]),
        pltpu.make_async_copy(other, total.at[pl.ds((1 - core) * half, half)], sem.at[1]),
    ]
    for copy in loads:
        copy.start()
    for copy in loads:
        copy.wait()
    modes = planes // 2
    sub = 8
    chunks = width // sub
    stepped[...] = probe_ref[...] - total[...] * scale

    block = 3
    sums[...] = jnp.zeros_like(sums)
    for jb in range(0, modes, block):
        for kb in range(jb, modes, block):
            pairs = [
                (j, k) for j in range(jb, jb + block) for k in range(kb, kb + block) if j <= k
            ]

            def accumulate(chunk, carried):
                rows = pl.ds(pl.multiple_of(chunk * sub, sub), sub)
                left = {j: (stepped[2 * j, rows], stepped[2 * j + 1, rows]) for j in range(jb, jb + block)}
                right = {k: (stepped[2 * k, rows], stepped[2 * k + 1, rows]) for k in range(kb, kb + block)}
                out = []
                for (j, k), (acc_re, acc_im) in zip(pairs, carried):
                    (l_re, l_im), (r_re, r_im) = left[j], right[k]
                    out.append(
                        (
                            acc_re + l_re * r_re + l_im * r_im,
                            acc_im + l_re * r_im - l_im * r_re,
                        )
                    )
                return out

            zero = jnp.zeros((sub, width), f32)
            result = lax.fori_loop(
                0, chunks, accumulate, [(zero, zero) for _ in pairs], unroll=16
            )
            for (j, k), (acc_re, acc_im) in zip(pairs, result):
                s_re = jnp.sum(acc_re, axis=0, keepdims=True)
                s_im = jnp.sum(acc_im, axis=0, keepdims=True)
                sums[0, j, k : k + 1] = s_re
                sums[1, j, k : k + 1] = s_im
                if j != k:
                    sums[0, k, j : j + 1] = s_re
                    sums[1, k, j : j + 1] = -s_im
    side = sums.shape[1]
    ones = jnp.ones((sub, width), f32)
    for part in range(2):
        for j in range(modes):
            row = lax.dot_general(
                ones, sums[part, j], (((1,), (1,)), ((), ())),
                precision=lax.Precision.HIGHEST, preferred_element_type=f32,
            )
            gram[part, j : j + 1, 0:side] = row[0:1]

    row_id = lax.broadcasted_iota(jnp.int32, (side, width), 0)
    lane_id = lax.broadcasted_iota(jnp.int32, (side, width), 1)
    valid = (row_id < modes) & (lane_id < modes)
    eye = jnp.where((lane_id == row_id + side) & (row_id < modes), 1.0, 0.0)
    work_re = jnp.where(valid, gram[0], 0.0) + eye
    work_im = jnp.where(valid, gram[1], 0.0)
    for k in range(modes - 1):
        row_re = work_re[k : k + 1]
        row_im = work_im[k : k + 1]
        inverse = 1.0 / work_re[k : k + 1, k : k + 1]
        f_re = jnp.where(row_id[:, :1] > k, work_re[:, k : k + 1] * inverse, 0.0)
        f_im = jnp.where(row_id[:, :1] > k, work_im[:, k : k + 1] * inverse, 0.0)
        work_re, work_im = (
            work_re - (f_re * row_re - f_im * row_im),
            work_im - (f_re * row_im + f_im * row_re),
        )
    place = 0
    for k in range(modes):
        for j in range(k):
            coef[place] = jnp.broadcast_to(work_re[k : k + 1, side + j : side + j + 1], (sub, width))
            coef[place + 1] = jnp.broadcast_to(work_im[k : k + 1, side + j : side + j + 1], (sub, width))
            place += 2

    def combine(chunk, carry):
        rows = pl.ds(pl.multiple_of(chunk * sub, sub), sub)
        values = [stepped[i, rows] for i in range(planes)]
        place = 0
        for k in range(modes):
            acc_re, acc_im = values[2 * k], values[2 * k + 1]
            for j in range(k):
                c_re, c_im = coef[place], coef[place + 1]
                place += 2
                acc_re = acc_re + (c_re * values[2 * j] + c_im * values[2 * j + 1])
                acc_im = acc_im + (c_re * values[2 * j + 1] - c_im * values[2 * j])
            out_ref[2 * k, rows] = acc_re
            out_ref[2 * k + 1, rows] = acc_im
        return carry

    lax.fori_loop(0, chunks, combine, 0)


def orthogonalize(core, probe, mine, other, divisor):
    planes, width = probe.shape[0], probe.shape[-1]
    modes = planes // 2
    side = 16
    return pl.pallas_call(
        functools.partial(orthogonal_kernel, 1.0 / divisor),
        out_shape=shape(*probe.shape),
        in_specs=[SMEM, VMEM, ANY, ANY],
        out_specs=VMEM,
        scratch_shapes=[
            pltpu.VMEM(probe.shape, f32),
            pltpu.VMEM(probe.shape, f32),
            pltpu.VMEM((2, side, side, width), f32),
            pltpu.VMEM((2, side, width), f32),
            pltpu.VMEM((modes * (modes - 1), 8, width), f32),
            DMA((2,)),
        ],
        compiler_params=params(32),
        name="orthogonalize",
    )(core, probe, mine, other)


def moved(shard, axes, pairs):
    return lax.ppermute(shard, axes, pairs)


def shifted(size, by):
    return [(i, i + by) for i in range(size) if 0 <= i + by < size]


def shifted_both(rows, cols, by):
    return [
        (r * cols + c, (r + by) * cols + c + by)
        for r in range(rows)
        for c in range(cols)
        if 0 <= r + by < rows and 0 <= c + by < cols
    ]


def sum_share(keep, groups):
    members = len(groups[0])
    parts = keep.reshape(members, -1, keep.shape[-1])
    parts = lax.all_to_all(parts, ("row", "col"), 0, 0, axis_index_groups=groups)
    return jnp.sum(parts, axis=0)


def gather_shares(share, groups):
    members = len(groups[0])
    parts = jnp.broadcast_to(share[None], (members,) + share.shape)
    return lax.all_to_all(parts, ("row", "col"), 0, 0, axis_index_groups=groups)


def local(object_slices, probe, measured, positions, counts):
    rows, cols = lax.axis_size("row"), lax.axis_size("col")
    modes, width = probe.shape[0], probe.shape[-1]
    planes = probe.reshape(2 * modes, width, width)
    capacity = positions.shape[2]
    spots = positions[:, 0]
    core = (lax.axis_index("row") % 2).astype(jnp.int32).reshape(1, 1)
    left_one, right_one = shifted(cols, -1), shifted(cols, 1)
    up_one, down_one = shifted(rows, -1), shifted(rows, 1)
    swap = [(r, r ^ 1) for r in range(rows)]
    groups = core_groups(rows, cols, 2)

    edge = object_slices[:, :, :, :width]
    first = width + 32
    second = (first + edge.shape[2]) // 2
    right = [
        moved(edge[:, :, begin:end], "col", left_one)
        for begin, end in ((0, first), (first, second), (second, edge.shape[2]))
    ]
    below = [moved(object_slices[s : s + 1, :, :width, :], "row", up_one) for s in range(2)]
    corner = moved(right[0][:, :, :width], "row", up_one)
    tables = [jnp.asarray(t) for t in make_tables(width)]
    probe_sum, terms, below_sum = near_slots(
        counts, spots, object_slices, below, planes, measured[0], tables, 1
    )
    keep, give, right_top, right_rest, *below_grads, corner_grad, terms = far_slots(
        counts, spots, core, object_slices, (*right, *below, corner), planes, measured[0],
        tables, (probe_sum, below_sum, terms),
    )
    keep = keep + moved(give, "row", swap)
    left_rest = moved(right_rest, "col", right_one)
    from_corner = moved(corner_grad, ("row", "col"), shifted_both(rows, cols, 1))
    left_top = moved(right_top, "col", right_one)
    above = [moved(part, "row", down_one) for part in below_grads]
    share = sum_share(keep, groups)
    mine = gather_shares(share, groups).reshape(keep.shape)
    object_next = settle(counts, spots, object_slices, terms, (left_top, left_rest), above, from_corner)
    mine, object_next = lax.optimization_barrier((mine, object_next))
    other = moved(mine, "row", swap)
    divisor = math.sqrt(rows * cols * capacity)
    probe_next = orthogonalize(core, planes, mine, other, divisor).reshape(probe.shape)
    return (object_next, probe_next)


def solution(mesh):
    return jax.shard_map(
        local,
        mesh=mesh,
        in_specs=(
            P(None, None, "row", "col"),
            P(),
            P("row", "col", None, None),
            P(None, "row", "col"),
            P("row", "col"),
        ),
        out_specs=(P(None, None, "row", "col"), P()),
        check_vma=False,
    )
```

```python
import functools
import math

import jax
import jax.numpy as jnp
import numpy as np
from jax import lax
from jax.experimental import pallas as pl
from jax.experimental.pallas import tpu as pltpu
from jax.sharding import PartitionSpec as P

FRESNEL = 40.0
f32 = jnp.float32
bf16 = jnp.bfloat16


def complex_block(matrix):
    return np.block([[matrix.real, matrix.imag], [-matrix.imag, matrix.real]])


def split_table(block):
    block = block.astype(np.float32)
    high = block.astype(jnp.bfloat16)
    low = (block - high.astype(np.float32)).astype(jnp.bfloat16)
    return np.stack([high, low])


def make_tables(width):
    index = np.arange(width)
    fourier = np.exp(-2j * np.pi / width * (index[:, None] * index[None, :] % width)) / np.sqrt(width)
    frequency = np.where(index < width // 2, index, index - width) / width
    chirp = np.exp(-1j * FRESNEL * frequency**2)
    spread = fourier.conj() @ (chirp[:, None] * fourier)
    forward = complex_block(fourier)
    step = complex_block(spread)
    steps = np.stack([split_table(step), split_table(step.T)])
    transforms = np.stack([split_table(forward), split_table(forward.T)])
    return steps, transforms


def split(values):
    high = values.astype(bf16)
    low = (values - high.astype(f32)).astype(bf16)
    return high, low


def mm(left, right):
    return jnp.dot(left, right, preferred_element_type=f32)


def times_right(planes, table):
    a_re, a_im, b_re, b_im = planes
    stacked = jnp.concatenate(
        [jnp.concatenate([a_re, a_im], axis=1), jnp.concatenate([b_re, b_im], axis=1)], axis=0
    )
    high, low = split(stacked)
    out = mm(high, table[0]) + mm(low, table[0]) + mm(high, table[1])
    w = a_re.shape[0]
    return out[:w, :w], out[:w, w:], out[w:, :w], out[w:, w:]


def times_left(planes, table):
    a_re, a_im, b_re, b_im = planes
    stacked = jnp.concatenate(
        [jnp.concatenate([a_re, b_re], axis=1), jnp.concatenate([a_im, b_im], axis=1)], axis=0
    )
    high, low = split(stacked)
    both = mm(jnp.concatenate([table[0], table[1]], axis=0), high)
    side = stacked.shape[0]
    out = both[:side] + both[side:] + mm(table[0], low)
    w = a_re.shape[0]
    return out[:w, :w], out[w:, :w], out[:w, w:], out[w:, w:]


def cmul(planes, re, im):
    a_re, a_im, b_re, b_im = planes
    return (
        a_re * re - a_im * im,
        a_re * im + a_im * re,
        b_re * re - b_im * im,
        b_re * im + b_im * re,
    )


def cmul_conj(planes, re, im):
    a_re, a_im, b_re, b_im = planes
    return (
        a_re * re + a_im * im,
        a_im * re - a_re * im,
        b_re * re + b_im * im,
        b_im * re - b_re * im,
    )


def overlap(wave, grad):
    re = wave[0] * grad[0] + wave[1] * grad[1] + wave[2] * grad[2] + wave[3] * grad[3]
    im = wave[0] * grad[1] - wave[1] * grad[0] + wave[2] * grad[3] - wave[3] * grad[2]
    return re, im


RIGHT, LEFT = 0, 1


def start_all(pairs, sems):
    copies = [pltpu.make_async_copy(src, dst, sems.at[i]) for i, (src, dst) in enumerate(pairs)]
    for copy in copies:
        copy.start()
    return copies


def near_sheet(tile, below, sheet, width):
    rows, cols = tile.shape[2:]
    down, across = pl.ds(rows, width), pl.ds(0, cols)
    return [(tile, sheet.at[:, :, pl.ds(0, rows), across])] + [
        (part, sheet.at[pl.ds(s, 1), :, down, across]) for s, part in enumerate(below)
    ]


def far_sheet(tile, right, below, corner, sheet, width):
    rows, cols = tile.shape[2:]
    down, across, last = pl.ds(rows, width), pl.ds(cols, width), pl.ds(cols - width, width)
    return (
        [(tile.at[:, :, :, last], sheet.at[:, :, pl.ds(0, rows), last])]
        + [(part, sheet.at[:, :, pl.ds(r, part.shape[2]), across]) for r, part in right]
        + [
            (part.at[:, :, :, last], sheet.at[pl.ds(s, 1), :, down, last])
            for s, part in enumerate(below)
        ]
        + [(corner, sheet.at[:, :, down, across])]
    )


def corner_of(pos_ref, slot, width):
    top = pos_ref[0, slot]
    left = pos_ref[1, slot]
    top8 = pl.multiple_of((top // 8) * 8, 8)
    left128 = pl.multiple_of((left // width) * width, width)
    return top8, left128, top - top8, left - left128


def cut_window(sheet, layer, plane, corner, width):
    top8, left128, drop_r, drop_c = corner
    wide = sheet[layer, plane, pl.ds(top8, width + 8), pl.ds(left128, 2 * width)]
    wide = pltpu.roll(wide, 2 * width - drop_c, 1)[:, :width]
    return pltpu.roll(wide, width + 8 - drop_r, 0)[:width]


def load4(ref, pair):
    return tuple(ref[pair * 4 + i] for i in range(4))


def store4(ref, pair, values):
    for i in range(4):
        ref[pair * 4 + i] = values[i]


def subtract_terms(slot, pos_ref, terms, sheet, width):
    top8, left128, drop_r, drop_c = corner_of(pos_ref, slot, width)
    for s in range(2):
        for c in range(2):
            wide = jnp.concatenate([terms[slot, s, c], jnp.zeros((8, width), f32)], axis=0)
            wide = pltpu.roll(wide, drop_r, 0)
            wide = jnp.concatenate([wide, jnp.zeros_like(wide)], axis=1)
            wide = pltpu.roll(wide, drop_c, 1)
            where = (s, c, pl.ds(top8, width + 8), pl.ds(left128, 2 * width))
            sheet[where] = sheet[where] - wide


def visit_slots(
    chosen, count, pos_ref, leaves, term_out, sheet, outer, probe, patterns, steps, transforms,
    window, wave, far, inten, pgrad, terms, sem_term,
):
    width = probe.shape[-1]
    pairs = probe.shape[0] // 4

    def save(slot):
        return pltpu.make_async_copy(terms.at[slot], term_out.at[slot], sem_term.at[slot])

    def process(slot):
        place = corner_of(pos_ref, slot, width)
        for s in range(2):
            for c in range(2):
                window[s, c] = cut_window(sheet, s, c, place, width)
        waves = [cmul(load4(probe, p), window[0, 0], window[0, 1]) for p in range(pairs)]
        waves = [times_right(v, steps[RIGHT]) for v in waves]
        waves = [times_left(v, steps[LEFT]) for v in waves]
        for p, v in enumerate(waves):
            store4(wave, p, v)
        waves = [cmul(v, window[1, 0], window[1, 1]) for v in waves]
        waves = [times_right(v, transforms[RIGHT]) for v in waves]
        waves = [times_left(v, transforms[LEFT]) for v in waves]
        total = -patterns[slot]
        for p, v in enumerate(waves):
            store4(far, p, v)
            total = total + (v[0] * v[0] + v[1] * v[1] + v[2] * v[2] + v[3] * v[3])
        inten[...] = total

        residual = inten[...]
        grads = [tuple(residual * x for x in load4(far, p)) for p in range(pairs)]
        grads = [times_right(v, transforms[LEFT]) for v in grads]
        grads = [times_left(v, transforms[RIGHT]) for v in grads]
        products = [overlap(load4(wave, p), v) for p, v in enumerate(grads)]
        terms[slot, 1, 0] = sum(t[0] for t in products)
        terms[slot, 1, 1] = sum(t[1] for t in products)
        grads = [cmul_conj(v, window[1, 0], window[1, 1]) for v in grads]
        grads = [times_right(v, steps[LEFT]) for v in grads]
        grads = [times_left(v, steps[RIGHT]) for v in grads]
        products = [overlap(load4(probe, p), v) for p, v in enumerate(grads)]
        terms[slot, 0, 0] = sum(t[0] for t in products)
        terms[slot, 0, 1] = sum(t[1] for t in products)
        grads = [cmul_conj(v, window[0, 0], window[0, 1]) for v in grads]
        for p, v in enumerate(grads):
            for i in range(4):
                pgrad[p * 4 + i] += v[i]
        save(slot).start()

        @pl.when(leaves(slot))
        def _():
            subtract_terms(slot, pos_ref, terms, outer, width)

    def visit(slot, carry):
        pl.when(chosen(slot))(lambda: process(slot))
        return carry

    def finish(slot, carry):
        pl.when(chosen(slot))(lambda: save(slot).wait())
        return carry

    lax.fori_loop(0, count, visit, 0)
    return lambda: lax.fori_loop(0, count, finish, 0)


def near_kernel(
    count_ref, pos_ref, tile, below_first, below_second, probe_in, pattern_in, step_in,
    transform_in,
    pgrad_out, term_out, below_out,
    sheet, outer, probe, patterns, steps, transforms, window, wave, far, inten, pgrad, terms,
    sem_in, sem_term, sem_out,
):
    width = probe.shape[-1]
    rows, cols = tile.shape[2:]
    loads = start_all(
        near_sheet(tile, (below_first, below_second), sheet, width)
        + [(probe_in, probe), (step_in, steps), (transform_in, transforms), (pattern_in, patterns)],
        sem_in,
    )
    outside = outer.at[:, :, pl.ds(rows, width), pl.ds(0, cols)]
    pgrad[...] = jnp.zeros_like(pgrad)
    outside[...] = jnp.zeros((2, 2, width, cols), f32)
    for copy in loads:
        copy.wait()
    wait_terms = visit_slots(
        lambda slot: pos_ref[1, slot] <= cols - width, count_ref[0, 0], pos_ref,
        lambda slot: pos_ref[0, slot] > rows - width,
        term_out, sheet, outer, probe, patterns, steps, transforms, window, wave, far, inten,
        pgrad, terms, sem_term,
    )
    stores = start_all([(pgrad, pgrad_out), (outside, below_out)], sem_out)
    wait_terms()
    for copy in stores:
        copy.wait()


def far_kernel(
    count_ref, pos_ref, core_ref, tile, top, middle, bottom, below_first, below_second, corner, probe_in,
    pattern_in, step_in, transform_in, pgrad_in, below_in, term_in,
    keep_out, give_out, right_top_out, right_rest_out, below_first_out, below_second_out,
    corner_out, term_out,
    sheet, outer, probe, patterns, steps, transforms, window, wave, far, inten, pgrad, terms,
    sem_in, sem_term, sem_out,
):
    width = probe.shape[-1]
    planes = probe.shape[0]
    rows, cols = tile.shape[2:]
    down, across, inner = pl.ds(rows, width), pl.ds(cols, width), pl.ds(0, cols)
    right = [(0, top), (top.shape[2], middle), (rows - bottom.shape[2], bottom)]
    loads = start_all(
        far_sheet(tile, right, (below_first, below_second), corner, sheet, width)
        + [(probe_in, probe), (step_in, steps), (transform_in, transforms), (pattern_in, patterns)]
        + [(pgrad_in, pgrad), (below_in, outer.at[:, :, down, inner])],
        sem_in,
    )
    outer[:, :, 0 : rows + width, cols : cols + width] = jnp.zeros((2, 2, rows + width, width), f32)
    for copy in loads:
        copy.wait()
    wait_terms = visit_slots(
        lambda slot: pos_ref[1, slot] > cols - width, count_ref[0, 0], pos_ref,
        lambda slot: pos_ref[1, slot] > cols - width,
        term_out, sheet, outer, probe, patterns, steps, transforms, window, wave, far, inten,
        pgrad, terms, sem_term,
    )
    half = planes // 2
    core = core_ref[0, 0]
    stores = start_all(
        [
            (pgrad.at[pl.ds((1 - core) * half, half)], give_out),
            (pgrad.at[pl.ds(core * half, half)], keep_out),
            (outer.at[:, :, down, across], corner_out),
            (outer.at[:, :, pl.ds(width, rows - width), across], right_rest_out),
            (outer.at[:, :, pl.ds(0, width), across], right_top_out),
            (outer.at[pl.ds(0, 1), :, down, inner], below_first_out),
            (outer.at[pl.ds(1, 1), :, down, inner], below_second_out),
        ],
        sem_out,
    )
    wait_terms()
    for copy in stores:
        copy.wait()


def load_terms(count, term_in, terms, sems):
    def fetch(slot):
        return pltpu.make_async_copy(term_in.at[slot], terms.at[slot], sems.at[slot])

    def begin(slot, carry):
        fetch(slot).start()
        return carry

    def finish(slot, carry):
        fetch(slot).wait()
        return carry

    lax.fori_loop(0, count, begin, 0)
    return lambda: lax.fori_loop(0, count, finish, 0)


def inside_kernel(count_ref, pos_ref, tile, term_in, tile_out, sheet, terms, sem_term, sems):
    width = terms.shape[-1]
    rows, cols = tile.shape[2:]
    count = count_ref[0, 0]
    inner = sheet.at[:, :, pl.ds(0, rows), pl.ds(0, cols)]
    load = pltpu.make_async_copy(tile, inner, sems.at[0])
    load.start()
    wait = load_terms(count, term_in, terms, sem_term)
    load.wait()
    wait()

    def visit(slot, carry):
        subtract_terms(slot, pos_ref, terms, sheet, width)
        return carry

    lax.fori_loop(0, count, visit, 0)
    store = pltpu.make_async_copy(inner, tile_out, sems.at[1])
    store.start()
    store.wait()


def settle_kernel(
    partial, left_top_in, left_rest_in, above_first_in, above_second_in, corner_in, tile_out,
    side, head, left, above, corner, sem_in, sem_out,
):
    width = corner_in.shape[-1]
    rows, cols = partial.shape[2:]
    edge, rest = pl.ds(0, width), pl.ds(width, cols - width)
    loads = start_all(
        [
            (partial.at[:, :, :, edge], side),
            (partial.at[:, :, edge, rest], head),
            (left_top_in, left.at[:, :, pl.ds(0, width)]),
            (left_rest_in, left.at[:, :, pl.ds(width, rows - width)]),
            (above_first_in, above.at[pl.ds(0, 1)]),
            (above_second_in, above.at[pl.ds(1, 1)]),
            (corner_in, corner),
        ],
        sem_in,
    )
    for copy in loads:
        copy.wait()
    side[...] += left[...]
    side[:, :, 0:width] += above[:, :, :, 0:width] + corner[...]
    head[...] += above[:, :, :, width:cols]
    stores = start_all(
        [(side, tile_out.at[:, :, :, edge]), (head, tile_out.at[:, :, edge, rest])], sem_out
    )
    for copy in stores:
        copy.wait()


VMEM = pl.BlockSpec(memory_space=pltpu.VMEM)
SMEM = pl.BlockSpec(memory_space=pltpu.SMEM)
ANY = pl.BlockSpec(memory_space=pl.ANY)
DMA = pltpu.SemaphoreType.DMA


def shape(*dims):
    return jax.ShapeDtypeStruct(dims, f32)


def params(mib):
    return pltpu.CompilerParams(vmem_limit_bytes=mib * 1024 * 1024)


def work(products):
    return pl.CostEstimate(
        flops=products * 2 * 256**3, bytes_accessed=8 * 1024 * 1024, transcendentals=0
    )


def slot_scratch(rows, cols, capacity, probe, steps, transforms, loads, stores):
    width = probe.shape[-1]
    stack = pltpu.VMEM(probe.shape, f32)
    field = pltpu.VMEM((2, 2, rows + width + 8, cols + 2 * width), f32)
    return [
        field,
        field,
        stack,
        pltpu.VMEM((capacity, width, width), f32),
        pltpu.VMEM(steps.shape, bf16),
        pltpu.VMEM(transforms.shape, bf16),
        pltpu.VMEM((2, 2, width, width), f32),
        stack,
        stack,
        pltpu.VMEM((width, width), f32),
        stack,
        pltpu.VMEM((capacity, 2, 2, width, width), f32),
        DMA((loads,)),
        DMA((capacity,)),
        DMA((stores,)),
    ]


def near_slots(counts, positions, tile, below, probe, patterns, tables, products):
    width = probe.shape[-1]
    rows, cols = tile.shape[2:]
    capacity = positions.shape[1]
    return pl.pallas_call(
        near_kernel,
        out_shape=[
            shape(*probe.shape),
            shape(capacity, 2, 2, width, width),
            shape(2, 2, width, cols),
        ],
        in_specs=[SMEM, SMEM] + [ANY] * 7,
        out_specs=[ANY] * 3,
        scratch_shapes=slot_scratch(rows, cols, capacity, probe, *tables, 7, 2),
        compiler_params=params(60),
        cost_estimate=work(products),
        name="near_slots",
    )(counts, positions, tile, *below, probe, patterns, *tables)


def far_slots(counts, positions, core, tile, halo, probe, patterns, tables, sums):
    planes, width = probe.shape[0], probe.shape[-1]
    rows, cols = tile.shape[2:]
    capacity = positions.shape[1]
    half = shape(planes // 2, width, width)
    return pl.pallas_call(
        far_kernel,
        out_shape=[
            half,
            half,
            shape(2, 2, width, width),
            shape(2, 2, rows - width, width),
            shape(1, 2, width, cols),
            shape(1, 2, width, cols),
            shape(2, 2, width, width),
            shape(capacity, 2, 2, width, width),
        ],
        in_specs=[SMEM, SMEM, SMEM] + [ANY] * 14,
        out_specs=[ANY] * 8,
        scratch_shapes=slot_scratch(rows, cols, capacity, probe, *tables, 13, 7),
        input_output_aliases={16: 7},
        compiler_params=params(60),
        cost_estimate=work(4 * capacity * planes),
        name="far_slots",
    )(counts, positions, core, tile, *halo, probe, patterns, *tables, *sums)


def inside(counts, positions, tile, terms):
    capacity, width = terms.shape[0], terms.shape[-1]
    rows, cols = tile.shape[2:]
    return pl.pallas_call(
        inside_kernel,
        out_shape=shape(*tile.shape),
        in_specs=[SMEM, SMEM, ANY, ANY],
        out_specs=ANY,
        scratch_shapes=[
            pltpu.VMEM((2, 2, rows + width + 8, cols + 2 * width), f32),
            pltpu.VMEM(terms.shape, f32),
            DMA((capacity,)),
            DMA((2,)),
        ],
        compiler_params=params(60),
        cost_estimate=work(8),
        name="inside",
    )(counts, positions, tile, terms)


def settle(partial, left, above, corner):
    width = corner.shape[-1]
    rows, cols = partial.shape[2:]
    return pl.pallas_call(
        settle_kernel,
        out_shape=shape(*partial.shape),
        in_specs=[ANY] * 6,
        out_specs=ANY,
        scratch_shapes=[
            pltpu.VMEM((2, 2, rows, width), f32),
            pltpu.VMEM((2, 2, width, cols - width), f32),
            pltpu.VMEM((2, 2, rows, width), f32),
            pltpu.VMEM((2, 2, width, cols), f32),
            pltpu.VMEM(corner.shape, f32),
            DMA((7,)),
            DMA((2,)),
        ],
        input_output_aliases={0: 0},
        compiler_params=params(60),
        cost_estimate=work(4096),
        name="settle",
    )(partial, *left, *above, corner)


def core_groups(rows, cols, split):
    return [
        [r * cols + c for r in range(part, rows, split) for c in range(cols)]
        for part in range(split)
    ]


def orthogonal_kernel(
    scale, core_ref, probe_ref, mine, other, out_ref, total, stepped, sums, gram, coef, sem
):
    planes, width = probe_ref.shape[0], probe_ref.shape[-1]
    half = planes // 2
    core = core_ref[0, 0]
    loads = [
        pltpu.make_async_copy(mine, total.at[pl.ds(core * half, half)], sem.at[0]),
        pltpu.make_async_copy(other, total.at[pl.ds((1 - core) * half, half)], sem.at[1]),
    ]
    for copy in loads:
        copy.start()
    for copy in loads:
        copy.wait()
    modes = planes // 2
    sub = 8
    chunks = width // sub
    stepped[...] = probe_ref[...] - total[...] * scale

    block = 3
    sums[...] = jnp.zeros_like(sums)
    for jb in range(0, modes, block):
        for kb in range(jb, modes, block):
            pairs = [
                (j, k) for j in range(jb, jb + block) for k in range(kb, kb + block) if j <= k
            ]

            def accumulate(chunk, carried):
                rows = pl.ds(pl.multiple_of(chunk * sub, sub), sub)
                left = {j: (stepped[2 * j, rows], stepped[2 * j + 1, rows]) for j in range(jb, jb + block)}
                right = {k: (stepped[2 * k, rows], stepped[2 * k + 1, rows]) for k in range(kb, kb + block)}
                out = []
                for (j, k), (acc_re, acc_im) in zip(pairs, carried):
                    (l_re, l_im), (r_re, r_im) = left[j], right[k]
                    out.append(
                        (
                            acc_re + l_re * r_re + l_im * r_im,
                            acc_im + l_re * r_im - l_im * r_re,
                        )
                    )
                return out

            zero = jnp.zeros((sub, width), f32)
            result = lax.fori_loop(
                0, chunks, accumulate, [(zero, zero) for _ in pairs], unroll=16
            )
            for (j, k), (acc_re, acc_im) in zip(pairs, result):
                s_re = jnp.sum(acc_re, axis=0, keepdims=True)
                s_im = jnp.sum(acc_im, axis=0, keepdims=True)
                sums[0, j, k : k + 1] = s_re
                sums[1, j, k : k + 1] = s_im
                if j != k:
                    sums[0, k, j : j + 1] = s_re
                    sums[1, k, j : j + 1] = -s_im
    side = sums.shape[1]
    ones = jnp.ones((sub, width), f32)
    for part in range(2):
        for j in range(modes):
            row = lax.dot_general(
                ones, sums[part, j], (((1,), (1,)), ((), ())),
                precision=lax.Precision.HIGHEST, preferred_element_type=f32,
            )
            gram[part, j : j + 1, 0:side] = row[0:1]

    row_id = lax.broadcasted_iota(jnp.int32, (side, width), 0)
    lane_id = lax.broadcasted_iota(jnp.int32, (side, width), 1)
    valid = (row_id < modes) & (lane_id < modes)
    eye = jnp.where((lane_id == row_id + side) & (row_id < modes), 1.0, 0.0)
    work_re = jnp.where(valid, gram[0], 0.0) + eye
    work_im = jnp.where(valid, gram[1], 0.0)
    for k in range(modes - 1):
        row_re = work_re[k : k + 1]
        row_im = work_im[k : k + 1]
        inverse = 1.0 / work_re[k : k + 1, k : k + 1]
        f_re = jnp.where(row_id[:, :1] > k, work_re[:, k : k + 1] * inverse, 0.0)
        f_im = jnp.where(row_id[:, :1] > k, work_im[:, k : k + 1] * inverse, 0.0)
        work_re, work_im = (
            work_re - (f_re * row_re - f_im * row_im),
            work_im - (f_re * row_im + f_im * row_re),
        )
    place = 0
    for k in range(modes):
        for j in range(k):
            coef[place] = jnp.broadcast_to(work_re[k : k + 1, side + j : side + j + 1], (sub, width))
            coef[place + 1] = jnp.broadcast_to(work_im[k : k + 1, side + j : side + j + 1], (sub, width))
            place += 2

    def combine(chunk, carry):
        rows = pl.ds(pl.multiple_of(chunk * sub, sub), sub)
        values = [stepped[i, rows] for i in range(planes)]
        place = 0
        for k in range(modes):
            acc_re, acc_im = values[2 * k], values[2 * k + 1]
            for j in range(k):
                c_re, c_im = coef[place], coef[place + 1]
                place += 2
                acc_re = acc_re + (c_re * values[2 * j] + c_im * values[2 * j + 1])
                acc_im = acc_im + (c_re * values[2 * j + 1] - c_im * values[2 * j])
            out_ref[2 * k, rows] = acc_re
            out_ref[2 * k + 1, rows] = acc_im
        return carry

    lax.fori_loop(0, chunks, combine, 0)


def orthogonalize(core, probe, mine, other, divisor):
    planes, width = probe.shape[0], probe.shape[-1]
    modes = planes // 2
    side = 16
    return pl.pallas_call(
        functools.partial(orthogonal_kernel, 1.0 / divisor),
        out_shape=shape(*probe.shape),
        in_specs=[SMEM, VMEM, ANY, ANY],
        out_specs=VMEM,
        scratch_shapes=[
            pltpu.VMEM(probe.shape, f32),
            pltpu.VMEM(probe.shape, f32),
            pltpu.VMEM((2, side, side, width), f32),
            pltpu.VMEM((2, side, width), f32),
            pltpu.VMEM((modes * (modes - 1), 8, width), f32),
            DMA((2,)),
        ],
        compiler_params=params(32),
        name="orthogonalize",
    )(core, probe, mine, other)


def moved(shard, axes, pairs):
    return lax.ppermute(shard, axes, pairs)


def shifted(size, by):
    return [(i, i + by) for i in range(size) if 0 <= i + by < size]


def shifted_both(rows, cols, by):
    return [
        (r * cols + c, (r + by) * cols + c + by)
        for r in range(rows)
        for c in range(cols)
        if 0 <= r + by < rows and 0 <= c + by < cols
    ]


def sum_share(keep, groups):
    members = len(groups[0])
    parts = keep.reshape(members, -1, keep.shape[-1])
    parts = lax.all_to_all(parts, ("row", "col"), 0, 0, axis_index_groups=groups)
    return jnp.sum(parts, axis=0)


def gather_shares(share, groups):
    members = len(groups[0])
    parts = jnp.broadcast_to(share[None], (members,) + share.shape)
    return lax.all_to_all(parts, ("row", "col"), 0, 0, axis_index_groups=groups)


def local(object_slices, probe, measured, positions, counts):
    rows, cols = lax.axis_size("row"), lax.axis_size("col")
    modes, width = probe.shape[0], probe.shape[-1]
    planes = probe.reshape(2 * modes, width, width)
    capacity = positions.shape[2]
    spots = positions[:, 0]
    core = (lax.axis_index("row") % 2).astype(jnp.int32).reshape(1, 1)
    left_one, right_one = shifted(cols, -1), shifted(cols, 1)
    up_one, down_one = shifted(rows, -1), shifted(rows, 1)
    swap = [(r, r ^ 1) for r in range(rows)]
    groups = core_groups(rows, cols, 2)

    edge = object_slices[:, :, :, :width]
    first = width + 32
    second = (first + edge.shape[2]) // 2
    right = [
        moved(edge[:, :, begin:end], "col", left_one)
        for begin, end in ((0, first), (first, second), (second, edge.shape[2]))
    ]
    below = [moved(object_slices[s : s + 1, :, :width, :], "row", up_one) for s in range(2)]
    corner = moved(right[0][:, :, :width], "row", up_one)
    tables = [jnp.asarray(t) for t in make_tables(width)]
    probe_sum, terms, below_sum = near_slots(
        counts, spots, object_slices, below, planes, measured[0], tables, 1
    )
    keep, give, right_top, right_rest, *below_grads, corner_grad, terms = far_slots(
        counts, spots, core, object_slices, (*right, *below, corner), planes, measured[0],
        tables, (probe_sum, below_sum, terms),
    )
    keep = keep + moved(give, "row", swap)
    left_rest = moved(right_rest, "col", right_one)
    from_corner = moved(corner_grad, ("row", "col"), shifted_both(rows, cols, 1))
    left_top = moved(right_top, "col", right_one)
    above = [moved(part, "row", down_one) for part in below_grads]
    share = sum_share(keep, groups)
    mine = gather_shares(share, groups).reshape(keep.shape)
    partial = inside(counts, spots, object_slices, terms)
    object_next = settle(partial, (left_top, left_rest), above, from_corner)
    mine, object_next = lax.optimization_barrier((mine, object_next))
    other = moved(mine, "row", swap)
    divisor = math.sqrt(rows * cols * capacity)
    probe_next = orthogonalize(core, planes, mine, other, divisor).reshape(probe.shape)
    return (object_next, probe_next)


def solution(mesh):
    return jax.shard_map(
        local,
        mesh=mesh,
        in_specs=(
            P(None, None, "row", "col"),
            P(),
            P("row", "col", None, None),
            P(None, "row", "col"),
            P("row", "col"),
        ),
        out_specs=(P(None, None, "row", "col"), P()),
        check_vma=False,
    )
```

```python
import functools
import math

import jax
import jax.numpy as jnp
import numpy as np
from jax import lax
from jax.experimental import pallas as pl
from jax.experimental.pallas import tpu as pltpu
from jax.sharding import PartitionSpec as P

FRESNEL = 40.0
f32 = jnp.float32
bf16 = jnp.bfloat16


def complex_block(matrix):
    return np.block([[matrix.real, matrix.imag], [-matrix.imag, matrix.real]])


def split_table(block):
    block = block.astype(np.float32)
    high = block.astype(jnp.bfloat16)
    low = (block - high.astype(np.float32)).astype(jnp.bfloat16)
    return np.stack([high, low])


def make_tables(width):
    index = np.arange(width)
    fourier = np.exp(-2j * np.pi / width * (index[:, None] * index[None, :] % width)) / np.sqrt(width)
    frequency = np.where(index < width // 2, index, index - width) / width
    chirp = np.exp(-1j * FRESNEL * frequency**2)
    spread = fourier.conj() @ (chirp[:, None] * fourier)
    forward = complex_block(fourier)
    step = complex_block(spread)
    steps = np.stack([split_table(step), split_table(step.T)])
    transforms = np.stack([split_table(forward), split_table(forward.T)])
    return steps, transforms


def split(values):
    high = values.astype(bf16)
    low = (values - high.astype(f32)).astype(bf16)
    return high, low


def mm(left, right):
    return jnp.dot(left, right, preferred_element_type=f32)


def times_right(planes, table):
    a_re, a_im, b_re, b_im = planes
    stacked = jnp.concatenate(
        [jnp.concatenate([a_re, a_im], axis=1), jnp.concatenate([b_re, b_im], axis=1)], axis=0
    )
    high, low = split(stacked)
    out = mm(high, table[0]) + mm(low, table[0]) + mm(high, table[1])
    w = a_re.shape[0]
    return out[:w, :w], out[:w, w:], out[w:, :w], out[w:, w:]


def times_left(planes, table):
    a_re, a_im, b_re, b_im = planes
    stacked = jnp.concatenate(
        [jnp.concatenate([a_re, b_re], axis=1), jnp.concatenate([a_im, b_im], axis=1)], axis=0
    )
    high, low = split(stacked)
    both = mm(jnp.concatenate([table[0], table[1]], axis=0), high)
    side = stacked.shape[0]
    out = both[:side] + both[side:] + mm(table[0], low)
    w = a_re.shape[0]
    return out[:w, :w], out[w:, :w], out[:w, w:], out[w:, w:]


def cmul(planes, re, im):
    a_re, a_im, b_re, b_im = planes
    return (
        a_re * re - a_im * im,
        a_re * im + a_im * re,
        b_re * re - b_im * im,
        b_re * im + b_im * re,
    )


def cmul_conj(planes, re, im):
    a_re, a_im, b_re, b_im = planes
    return (
        a_re * re + a_im * im,
        a_im * re - a_re * im,
        b_re * re + b_im * im,
        b_im * re - b_re * im,
    )


def overlap(wave, grad):
    re = wave[0] * grad[0] + wave[1] * grad[1] + wave[2] * grad[2] + wave[3] * grad[3]
    im = wave[0] * grad[1] - wave[1] * grad[0] + wave[2] * grad[3] - wave[3] * grad[2]
    return re, im


RIGHT, LEFT = 0, 1


def start_all(pairs, sems):
    copies = [pltpu.make_async_copy(src, dst, sems.at[i]) for i, (src, dst) in enumerate(pairs)]
    for copy in copies:
        copy.start()
    return copies


def near_sheet(tile, below, sheet, width):
    rows, cols = tile.shape[2:]
    down, across = pl.ds(rows, width), pl.ds(0, cols)
    return [(tile, sheet.at[:, :, pl.ds(0, rows), across])] + [
        (part, sheet.at[pl.ds(s, 1), :, down, across]) for s, part in enumerate(below)
    ]


def far_sheet(tile, right, below, corner, sheet, width):
    rows, cols = tile.shape[2:]
    down, across, last = pl.ds(rows, width), pl.ds(cols, width), pl.ds(cols - width, width)
    return (
        [(tile.at[:, :, :, last], sheet.at[:, :, pl.ds(0, rows), last])]
        + [(part, sheet.at[:, :, pl.ds(r, part.shape[2]), across]) for r, part in right]
        + [
            (part.at[:, :, :, last], sheet.at[pl.ds(s, 1), :, down, last])
            for s, part in enumerate(below)
        ]
        + [(corner, sheet.at[:, :, down, across])]
    )


def corner_of(pos_ref, slot, width):
    top = pos_ref[0, slot]
    left = pos_ref[1, slot]
    top8 = pl.multiple_of((top // 8) * 8, 8)
    left128 = pl.multiple_of((left // width) * width, width)
    return top8, left128, top - top8, left - left128


def cut_window(sheet, layer, plane, corner, width):
    top8, left128, drop_r, drop_c = corner
    wide = sheet[layer, plane, pl.ds(top8, width + 8), pl.ds(left128, 2 * width)]
    wide = pltpu.roll(wide, 2 * width - drop_c, 1)[:, :width]
    return pltpu.roll(wide, width + 8 - drop_r, 0)[:width]


def load4(ref, pair):
    return tuple(ref[pair * 4 + i] for i in range(4))


def store4(ref, pair, values):
    for i in range(4):
        ref[pair * 4 + i] = values[i]


def subtract_terms(slot, pos_ref, terms, sheet, width):
    top8, left128, drop_r, drop_c = corner_of(pos_ref, slot, width)
    for s in range(2):
        for c in range(2):
            wide = jnp.concatenate([terms[slot, s, c], jnp.zeros((8, width), f32)], axis=0)
            wide = pltpu.roll(wide, drop_r, 0)
            wide = jnp.concatenate([wide, jnp.zeros_like(wide)], axis=1)
            wide = pltpu.roll(wide, drop_c, 1)
            where = (s, c, pl.ds(top8, width + 8), pl.ds(left128, 2 * width))
            sheet[where] = sheet[where] - wide


def visit_slots(
    chosen, count, pos_ref, leaves, term_out, sheet, outer, probe, patterns, steps, transforms,
    window, wave, far, inten, pgrad, terms, sem_term,
):
    width = probe.shape[-1]
    pairs = probe.shape[0] // 4

    def save(slot):
        return pltpu.make_async_copy(terms.at[slot], term_out.at[slot], sem_term.at[slot])

    def process(slot):
        place = corner_of(pos_ref, slot, width)
        for s in range(2):
            for c in range(2):
                window[s, c] = cut_window(sheet, s, c, place, width)
        waves = [cmul(load4(probe, p), window[0, 0], window[0, 1]) for p in range(pairs)]
        waves = [times_right(v, steps[RIGHT]) for v in waves]
        waves = [times_left(v, steps[LEFT]) for v in waves]
        for p, v in enumerate(waves):
            store4(wave, p, v)
        waves = [cmul(v, window[1, 0], window[1, 1]) for v in waves]
        waves = [times_right(v, transforms[RIGHT]) for v in waves]
        waves = [times_left(v, transforms[LEFT]) for v in waves]
        total = -patterns[slot]
        for p, v in enumerate(waves):
            store4(far, p, v)
            total = total + (v[0] * v[0] + v[1] * v[1] + v[2] * v[2] + v[3] * v[3])
        inten[...] = total

        residual = inten[...]
        grads = [tuple(residual * x for x in load4(far, p)) for p in range(pairs)]
        grads = [times_right(v, transforms[LEFT]) for v in grads]
        grads = [times_left(v, transforms[RIGHT]) for v in grads]
        products = [overlap(load4(wave, p), v) for p, v in enumerate(grads)]
        terms[slot, 1, 0] = sum(t[0] for t in products)
        terms[slot, 1, 1] = sum(t[1] for t in products)
        grads = [cmul_conj(v, window[1, 0], window[1, 1]) for v in grads]
        grads = [times_right(v, steps[LEFT]) for v in grads]
        grads = [times_left(v, steps[RIGHT]) for v in grads]
        products = [overlap(load4(probe, p), v) for p, v in enumerate(grads)]
        terms[slot, 0, 0] = sum(t[0] for t in products)
        terms[slot, 0, 1] = sum(t[1] for t in products)
        grads = [cmul_conj(v, window[0, 0], window[0, 1]) for v in grads]
        for p, v in enumerate(grads):
            for i in range(4):
                pgrad[p * 4 + i] += v[i]
        save(slot).start()

        @pl.when(leaves(slot))
        def _():
            subtract_terms(slot, pos_ref, terms, outer, width)

    def visit(slot, carry):
        pl.when(chosen(slot))(lambda: process(slot))
        return carry

    def finish(slot, carry):
        pl.when(chosen(slot))(lambda: save(slot).wait())
        return carry

    lax.fori_loop(0, count, visit, 0)
    return lambda: lax.fori_loop(0, count, finish, 0)


def near_kernel(
    count_ref, pos_ref, tile, below_first, below_second, probe_in, pattern_in, step_in,
    transform_in,
    pgrad_out, term_out, below_out,
    sheet, outer, probe, patterns, steps, transforms, window, wave, far, inten, pgrad, terms,
    sem_in, sem_term, sem_out,
):
    width = probe.shape[-1]
    rows, cols = tile.shape[2:]
    loads = start_all(
        near_sheet(tile, (below_first, below_second), sheet, width)
        + [(probe_in, probe), (step_in, steps), (transform_in, transforms), (pattern_in, patterns)],
        sem_in,
    )
    outside = outer.at[:, :, pl.ds(rows, width), pl.ds(0, cols)]
    pgrad[...] = jnp.zeros_like(pgrad)
    outside[...] = jnp.zeros((2, 2, width, cols), f32)
    for copy in loads:
        copy.wait()
    wait_terms = visit_slots(
        lambda slot: pos_ref[1, slot] <= cols - width, count_ref[0, 0], pos_ref,
        lambda slot: pos_ref[0, slot] > rows - width,
        term_out, sheet, outer, probe, patterns, steps, transforms, window, wave, far, inten,
        pgrad, terms, sem_term,
    )
    stores = start_all([(pgrad, pgrad_out), (outside, below_out)], sem_out)
    wait_terms()
    for copy in stores:
        copy.wait()


def far_kernel(
    count_ref, pos_ref, core_ref, tile, top, middle, bottom, below_first, below_second, corner, probe_in,
    pattern_in, step_in, transform_in, pgrad_in, below_in, term_in,
    keep_out, give_out, right_top_out, right_rest_out, below_first_out, below_second_out,
    corner_out, term_out,
    sheet, outer, probe, patterns, steps, transforms, window, wave, far, inten, pgrad, terms,
    sem_in, sem_term, sem_out,
):
    width = probe.shape[-1]
    planes = probe.shape[0]
    rows, cols = tile.shape[2:]
    down, across, inner = pl.ds(rows, width), pl.ds(cols, width), pl.ds(0, cols)
    right = [(0, top), (top.shape[2], middle), (rows - bottom.shape[2], bottom)]
    count = count_ref[0, 0]
    reaching = [
        ((slot < count) & (pos_ref[1, slot] > cols - width)).astype(jnp.int32)
        for slot in range(pos_ref.shape[1])
    ]
    needed = sum(reaching) > 0
    sums = [(pgrad_in, pgrad), (below_in, outer.at[:, :, down, inner])]
    inputs = far_sheet(tile, right, (below_first, below_second), corner, sheet, width) + [
        (probe_in, probe), (step_in, steps), (transform_in, transforms), (pattern_in, patterns)
    ]
    loads = [
        pltpu.make_async_copy(src, dst, sem_in.at[i]) for i, (src, dst) in enumerate(sums + inputs)
    ]
    kept, optional = loads[: len(sums)], loads[len(sums) :]

    @pl.when(needed)
    def _():
        for copy in optional:
            copy.start()

    for copy in kept:
        copy.start()
    outer[:, :, 0 : rows + width, cols : cols + width] = jnp.zeros((2, 2, rows + width, width), f32)
    for copy in kept:
        copy.wait()

    @pl.when(needed)
    def _():
        for copy in optional:
            copy.wait()

    wait_terms = visit_slots(
        lambda slot: pos_ref[1, slot] > cols - width, count_ref[0, 0], pos_ref,
        lambda slot: pos_ref[1, slot] > cols - width,
        term_out, sheet, outer, probe, patterns, steps, transforms, window, wave, far, inten,
        pgrad, terms, sem_term,
    )
    half = planes // 2
    core = core_ref[0, 0]
    stores = start_all(
        [
            (pgrad.at[pl.ds((1 - core) * half, half)], give_out),
            (pgrad.at[pl.ds(core * half, half)], keep_out),
            (outer.at[:, :, down, across], corner_out),
            (outer.at[:, :, pl.ds(width, rows - width), across], right_rest_out),
            (outer.at[:, :, pl.ds(0, width), across], right_top_out),
            (outer.at[pl.ds(0, 1), :, down, inner], below_first_out),
            (outer.at[pl.ds(1, 1), :, down, inner], below_second_out),
        ],
        sem_out,
    )
    wait_terms()
    for copy in stores:
        copy.wait()


def load_terms(count, term_in, terms, sems):
    def fetch(slot):
        return pltpu.make_async_copy(term_in.at[slot], terms.at[slot], sems.at[slot])

    def begin(slot, carry):
        fetch(slot).start()
        return carry

    def finish(slot, carry):
        fetch(slot).wait()
        return carry

    lax.fori_loop(0, count, begin, 0)
    return lambda: lax.fori_loop(0, count, finish, 0)


def inside_kernel(count_ref, pos_ref, tile, term_in, tile_out, sheet, terms, sem_term, sems):
    width = terms.shape[-1]
    rows, cols = tile.shape[2:]
    count = count_ref[0, 0]
    inner = sheet.at[:, :, pl.ds(0, rows), pl.ds(0, cols)]
    load = pltpu.make_async_copy(tile, inner, sems.at[0])
    load.start()
    wait = load_terms(count, term_in, terms, sem_term)
    load.wait()
    wait()

    def visit(slot, carry):
        subtract_terms(slot, pos_ref, terms, sheet, width)
        return carry

    lax.fori_loop(0, count, visit, 0)
    store = pltpu.make_async_copy(inner, tile_out, sems.at[1])
    store.start()
    store.wait()


def settle_kernel(
    partial, left_top_in, left_rest_in, above_first_in, above_second_in, corner_in, tile_out,
    side, head, left, above, corner, sem_in, sem_out,
):
    width = corner_in.shape[-1]
    rows, cols = partial.shape[2:]
    edge, rest = pl.ds(0, width), pl.ds(width, cols - width)
    loads = start_all(
        [
            (partial.at[:, :, :, edge], side),
            (partial.at[:, :, edge, rest], head),
            (left_top_in, left.at[:, :, pl.ds(0, width)]),
            (left_rest_in, left.at[:, :, pl.ds(width, rows - width)]),
            (above_first_in, above.at[pl.ds(0, 1)]),
            (above_second_in, above.at[pl.ds(1, 1)]),
            (corner_in, corner),
        ],
        sem_in,
    )
    for copy in loads:
        copy.wait()
    side[...] += left[...]
    side[:, :, 0:width] += above[:, :, :, 0:width] + corner[...]
    head[...] += above[:, :, :, width:cols]
    stores = start_all(
        [(side, tile_out.at[:, :, :, edge]), (head, tile_out.at[:, :, edge, rest])], sem_out
    )
    for copy in stores:
        copy.wait()


VMEM = pl.BlockSpec(memory_space=pltpu.VMEM)
SMEM = pl.BlockSpec(memory_space=pltpu.SMEM)
ANY = pl.BlockSpec(memory_space=pl.ANY)
DMA = pltpu.SemaphoreType.DMA


def shape(*dims):
    return jax.ShapeDtypeStruct(dims, f32)


def params(mib):
    return pltpu.CompilerParams(vmem_limit_bytes=mib * 1024 * 1024)


def work(products):
    return pl.CostEstimate(
        flops=products * 2 * 256**3, bytes_accessed=8 * 1024 * 1024, transcendentals=0
    )


def slot_scratch(rows, cols, capacity, probe, steps, transforms, loads, stores):
    width = probe.shape[-1]
    stack = pltpu.VMEM(probe.shape, f32)
    field = pltpu.VMEM((2, 2, rows + width + 8, cols + 2 * width), f32)
    return [
        field,
        field,
        stack,
        pltpu.VMEM((capacity, width, width), f32),
        pltpu.VMEM(steps.shape, bf16),
        pltpu.VMEM(transforms.shape, bf16),
        pltpu.VMEM((2, 2, width, width), f32),
        stack,
        stack,
        pltpu.VMEM((width, width), f32),
        stack,
        pltpu.VMEM((capacity, 2, 2, width, width), f32),
        DMA((loads,)),
        DMA((capacity,)),
        DMA((stores,)),
    ]


def near_slots(counts, positions, tile, below, probe, patterns, tables, products):
    width = probe.shape[-1]
    rows, cols = tile.shape[2:]
    capacity = positions.shape[1]
    return pl.pallas_call(
        near_kernel,
        out_shape=[
            shape(*probe.shape),
            shape(capacity, 2, 2, width, width),
            shape(2, 2, width, cols),
        ],
        in_specs=[SMEM, SMEM] + [ANY] * 7,
        out_specs=[ANY] * 3,
        scratch_shapes=slot_scratch(rows, cols, capacity, probe, *tables, 7, 2),
        compiler_params=params(60),
        cost_estimate=work(products),
        name="near_slots",
    )(counts, positions, tile, *below, probe, patterns, *tables)


def far_slots(counts, positions, core, tile, halo, probe, patterns, tables, sums):
    planes, width = probe.shape[0], probe.shape[-1]
    rows, cols = tile.shape[2:]
    capacity = positions.shape[1]
    half = shape(planes // 2, width, width)
    return pl.pallas_call(
        far_kernel,
        out_shape=[
            half,
            half,
            shape(2, 2, width, width),
            shape(2, 2, rows - width, width),
            shape(1, 2, width, cols),
            shape(1, 2, width, cols),
            shape(2, 2, width, width),
            shape(capacity, 2, 2, width, width),
        ],
        in_specs=[SMEM, SMEM, SMEM] + [ANY] * 14,
        out_specs=[ANY] * 8,
        scratch_shapes=slot_scratch(rows, cols, capacity, probe, *tables, 13, 7),
        input_output_aliases={16: 7},
        compiler_params=params(60),
        cost_estimate=work(4 * capacity * planes),
        name="far_slots",
    )(counts, positions, core, tile, *halo, probe, patterns, *tables, *sums)


def inside(counts, positions, tile, terms):
    capacity, width = terms.shape[0], terms.shape[-1]
    rows, cols = tile.shape[2:]
    return pl.pallas_call(
        inside_kernel,
        out_shape=shape(*tile.shape),
        in_specs=[SMEM, SMEM, ANY, ANY],
        out_specs=ANY,
        scratch_shapes=[
            pltpu.VMEM((2, 2, rows + width + 8, cols + 2 * width), f32),
            pltpu.VMEM(terms.shape, f32),
            DMA((capacity,)),
            DMA((2,)),
        ],
        compiler_params=params(60),
        cost_estimate=work(8),
        name="inside",
    )(counts, positions, tile, terms)


def settle(partial, left, above, corner):
    width = corner.shape[-1]
    rows, cols = partial.shape[2:]
    return pl.pallas_call(
        settle_kernel,
        out_shape=shape(*partial.shape),
        in_specs=[ANY] * 6,
        out_specs=ANY,
        scratch_shapes=[
            pltpu.VMEM((2, 2, rows, width), f32),
            pltpu.VMEM((2, 2, width, cols - width), f32),
            pltpu.VMEM((2, 2, rows, width), f32),
            pltpu.VMEM((2, 2, width, cols), f32),
            pltpu.VMEM(corner.shape, f32),
            DMA((7,)),
            DMA((2,)),
        ],
        input_output_aliases={0: 0},
        compiler_params=params(60),
        cost_estimate=work(4096),
        name="settle",
    )(partial, *left, *above, corner)


def core_groups(rows, cols, split):
    return [
        [r * cols + c for r in range(part, rows, split) for c in range(cols)]
        for part in range(split)
    ]


def orthogonal_kernel(
    scale, core_ref, probe_ref, mine, other, out_ref, total, stepped, sums, gram, coef, sem
):
    planes, width = probe_ref.shape[0], probe_ref.shape[-1]
    half = planes // 2
    core = core_ref[0, 0]
    loads = [
        pltpu.make_async_copy(mine, total.at[pl.ds(core * half, half)], sem.at[0]),
        pltpu.make_async_copy(other, total.at[pl.ds((1 - core) * half, half)], sem.at[1]),
    ]
    for copy in loads:
        copy.start()
    for copy in loads:
        copy.wait()
    modes = planes // 2
    sub = 8
    chunks = width // sub
    stepped[...] = probe_ref[...] - total[...] * scale

    block = 3
    sums[...] = jnp.zeros_like(sums)
    for jb in range(0, modes, block):
        for kb in range(jb, modes, block):
            pairs = [
                (j, k) for j in range(jb, jb + block) for k in range(kb, kb + block) if j <= k
            ]

            def accumulate(chunk, carried):
                rows = pl.ds(pl.multiple_of(chunk * sub, sub), sub)
                left = {j: (stepped[2 * j, rows], stepped[2 * j + 1, rows]) for j in range(jb, jb + block)}
                right = {k: (stepped[2 * k, rows], stepped[2 * k + 1, rows]) for k in range(kb, kb + block)}
                out = []
                for (j, k), (acc_re, acc_im) in zip(pairs, carried):
                    (l_re, l_im), (r_re, r_im) = left[j], right[k]
                    out.append(
                        (
                            acc_re + l_re * r_re + l_im * r_im,
                            acc_im + l_re * r_im - l_im * r_re,
                        )
                    )
                return out

            zero = jnp.zeros((sub, width), f32)
            result = lax.fori_loop(
                0, chunks, accumulate, [(zero, zero) for _ in pairs], unroll=16
            )
            for (j, k), (acc_re, acc_im) in zip(pairs, result):
                s_re = jnp.sum(acc_re, axis=0, keepdims=True)
                s_im = jnp.sum(acc_im, axis=0, keepdims=True)
                sums[0, j, k : k + 1] = s_re
                sums[1, j, k : k + 1] = s_im
                if j != k:
                    sums[0, k, j : j + 1] = s_re
                    sums[1, k, j : j + 1] = -s_im
    side = sums.shape[1]
    ones = jnp.ones((sub, width), f32)
    for part in range(2):
        for j in range(modes):
            row = lax.dot_general(
                ones, sums[part, j], (((1,), (1,)), ((), ())),
                precision=lax.Precision.HIGHEST, preferred_element_type=f32,
            )
            gram[part, j : j + 1, 0:side] = row[0:1]

    row_id = lax.broadcasted_iota(jnp.int32, (side, width), 0)
    lane_id = lax.broadcasted_iota(jnp.int32, (side, width), 1)
    valid = (row_id < modes) & (lane_id < modes)
    eye = jnp.where((lane_id == row_id + side) & (row_id < modes), 1.0, 0.0)
    work_re = jnp.where(valid, gram[0], 0.0) + eye
    work_im = jnp.where(valid, gram[1], 0.0)
    for k in range(modes - 1):
        row_re = work_re[k : k + 1]
        row_im = work_im[k : k + 1]
        inverse = 1.0 / work_re[k : k + 1, k : k + 1]
        f_re = jnp.where(row_id[:, :1] > k, work_re[:, k : k + 1] * inverse, 0.0)
        f_im = jnp.where(row_id[:, :1] > k, work_im[:, k : k + 1] * inverse, 0.0)
        work_re, work_im = (
            work_re - (f_re * row_re - f_im * row_im),
            work_im - (f_re * row_im + f_im * row_re),
        )
    place = 0
    for k in range(modes):
        for j in range(k):
            coef[place] = jnp.broadcast_to(work_re[k : k + 1, side + j : side + j + 1], (sub, width))
            coef[place + 1] = jnp.broadcast_to(work_im[k : k + 1, side + j : side + j + 1], (sub, width))
            place += 2

    def combine(chunk, carry):
        rows = pl.ds(pl.multiple_of(chunk * sub, sub), sub)
        values = [stepped[i, rows] for i in range(planes)]
        place = 0
        for k in range(modes):
            acc_re, acc_im = values[2 * k], values[2 * k + 1]
            for j in range(k):
                c_re, c_im = coef[place], coef[place + 1]
                place += 2
                acc_re = acc_re + (c_re * values[2 * j] + c_im * values[2 * j + 1])
                acc_im = acc_im + (c_re * values[2 * j + 1] - c_im * values[2 * j])
            out_ref[2 * k, rows] = acc_re
            out_ref[2 * k + 1, rows] = acc_im
        return carry

    lax.fori_loop(0, chunks, combine, 0)


def orthogonalize(core, probe, mine, other, divisor):
    planes, width = probe.shape[0], probe.shape[-1]
    modes = planes // 2
    side = 16
    return pl.pallas_call(
        functools.partial(orthogonal_kernel, 1.0 / divisor),
        out_shape=shape(*probe.shape),
        in_specs=[SMEM, VMEM, ANY, ANY],
        out_specs=VMEM,
        scratch_shapes=[
            pltpu.VMEM(probe.shape, f32),
            pltpu.VMEM(probe.shape, f32),
            pltpu.VMEM((2, side, side, width), f32),
            pltpu.VMEM((2, side, width), f32),
            pltpu.VMEM((modes * (modes - 1), 8, width), f32),
            DMA((2,)),
        ],
        compiler_params=params(32),
        name="orthogonalize",
    )(core, probe, mine, other)


def moved(shard, axes, pairs):
    return lax.ppermute(shard, axes, pairs)


def shifted(size, by):
    return [(i, i + by) for i in range(size) if 0 <= i + by < size]


def shifted_both(rows, cols, by):
    return [
        (r * cols + c, (r + by) * cols + c + by)
        for r in range(rows)
        for c in range(cols)
        if 0 <= r + by < rows and 0 <= c + by < cols
    ]


def sum_share(keep, groups):
    members = len(groups[0])
    parts = keep.reshape(members, -1, keep.shape[-1])
    parts = lax.all_to_all(parts, ("row", "col"), 0, 0, axis_index_groups=groups)
    return jnp.sum(parts, axis=0)


def gather_shares(share, groups):
    members = len(groups[0])
    parts = jnp.broadcast_to(share[None], (members,) + share.shape)
    return lax.all_to_all(parts, ("row", "col"), 0, 0, axis_index_groups=groups)


def local(object_slices, probe, measured, positions, counts):
    rows, cols = lax.axis_size("row"), lax.axis_size("col")
    modes, width = probe.shape[0], probe.shape[-1]
    planes = probe.reshape(2 * modes, width, width)
    capacity = positions.shape[2]
    spots = positions[:, 0]
    core = (lax.axis_index("row") % 2).astype(jnp.int32).reshape(1, 1)
    left_one, right_one = shifted(cols, -1), shifted(cols, 1)
    up_one, down_one = shifted(rows, -1), shifted(rows, 1)
    swap = [(r, r ^ 1) for r in range(rows)]
    groups = core_groups(rows, cols, 2)

    edge = object_slices[:, :, :, :width]
    first = width + 32
    second = (first + edge.shape[2]) // 2
    right = [
        moved(edge[:, :, begin:end], "col", left_one)
        for begin, end in ((0, first), (first, second), (second, edge.shape[2]))
    ]
    below = [moved(object_slices[s : s + 1, :, :width, :], "row", up_one) for s in range(2)]
    corner = moved(right[0][:, :, :width], "row", up_one)
    tables = [jnp.asarray(t) for t in make_tables(width)]
    probe_sum, terms, below_sum = near_slots(
        counts, spots, object_slices, below, planes, measured[0], tables, 1
    )
    keep, give, right_top, right_rest, *below_grads, corner_grad, terms = far_slots(
        counts, spots, core, object_slices, (*right, *below, corner), planes, measured[0],
        tables, (probe_sum, below_sum, terms),
    )
    keep = keep + moved(give, "row", swap)
    left_rest = moved(right_rest, "col", right_one)
    from_corner = moved(corner_grad, ("row", "col"), shifted_both(rows, cols, 1))
    left_top = moved(right_top, "col", right_one)
    above = [moved(part, "row", down_one) for part in below_grads]
    share = sum_share(keep, groups)
    mine = gather_shares(share, groups).reshape(keep.shape)
    partial = inside(counts, spots, object_slices, terms)
    object_next = settle(partial, (left_top, left_rest), above, from_corner)
    mine, object_next = lax.optimization_barrier((mine, object_next))
    other = moved(mine, "row", swap)
    divisor = math.sqrt(rows * cols * capacity)
    probe_next = orthogonalize(core, planes, mine, other, divisor).reshape(probe.shape)
    return (object_next, probe_next)


def solution(mesh):
    return jax.shard_map(
        local,
        mesh=mesh,
        in_specs=(
            P(None, None, "row", "col"),
            P(),
            P("row", "col", None, None),
            P(None, "row", "col"),
            P("row", "col"),
        ),
        out_specs=(P(None, None, "row", "col"), P()),
        check_vma=False,
    )
```
